256 devices in a mesh: lat: 8 (over x, core), lon: 32 (over z, y).
Axes of the slice: x: 4, y: 4, z: 8, core: 2. Of those that a mesh axis runs over, the one named last changes fastest.
Arguments:
- patches: bfloat16 [128, 1024, 512], P('lat', 'lon'), may hold values from -6 to 6
- patch_mask: int32 [128, 1024], P('lat', 'lon'), may hold values 0 or 1
- mask_token: bfloat16 [512], replicated, may hold values from -6 to 6
- w_qkv: bfloat16 [512, 1536], replicated, may hold values from -0.25 to 0.25
- w_proj: bfloat16 [512, 512], replicated, may hold values from -0.25 to 0.25
- logit_scale: float32 [16], replicated, may hold values from 2 to 20
- rel_bias: float32 [16, 64, 64], replicated, may hold values from -4 to 4
- attn_gain: float32 [512], replicated, may hold values from 0.1 to 1.9
- moe_gain: float32 [512], replicated, may hold values from 0.1 to 1.9
- router: bfloat16 [512, 32], replicated, may hold values from -0.5 to 0.5
- expert_ids: int32 [8, 32, 512, 1], P('lat', 'lon'), may hold values from 0 to 31; in each aligned block of 512 rows (0 to 511, 512 to 1023, ..., all dimensions but the last counted through in order) at most 32 rows name the same one
- w_in: bfloat16 [32, 512, 2048], P('lon'), may hold values from -0.25 to 0.25
- w_out: bfloat16 [32, 512, 2048], P('lon'), may hold values from -0.125 to 0.125
- cotangent: bfloat16 [128, 1024, 512], P('lat', 'lon'), may hold values from -6 to 6
Outputs:
- block_out: bfloat16 [128, 1024, 512], P('lat', 'lon')
- mixer_grad: float32 [128, 1024, 512], P('lat', 'lon')
- weight_grads: float32 [512, 32, 4096], P('lat', 'lon')
The draws below stay inside these ranges and needn't reach their ends.
Inputs may be any that keep to these rules, and one draw needn't show every extreme that they name: `expert_ids`: among the 512 patches of one device no expert is named more than 32 times.
All inputs are finite; a program needn't handle non-finite values. No bound on the sum of `patch_mask` on one device may be relied on, other than what follows from the above.
Results may differ from the reference program's by a relative error of at most 0.03.
Values may be sent and summed in bfloat16 or wider, within the bound.
No kernel may reach another device: no remote copies, remote signals or barrier semaphores. Data moves between devices by JAX's collectives and lax.ppermute only.
A program may use at most 128 MiB of HBM per device.

```python
import math
import jax
import jax.numpy as jnp
import numpy as np
from jax import lax

D = 512
HEADS = 16
WIN = 8
SHIFT = 4
FF = 2048
EXPERTS = 32
HL = 16
WL = 32
TOK_DEV = 512
CAP = 32
LAT = 128
LON = 1024
BANDS_LAT = 8
BANDS_LON = 32
N_LAT = 8
N_LON = 32


def set_ends(values, rng, low, high):
    shape = values.shape
    place = [jax.random.randint(jax.random.fold_in(rng, axis), (), 0, shape[axis]) for axis in range(len(shape))]
    values = values.at[tuple(place)].set(low)
    longest = shape.index(max(shape))
    place[longest] = (place[longest] + 1) % shape[longest]
    return values.at[tuple(place)].set(high)


def levels(own_key, shape, pieces, low, top_value):
    loudness = 1.0
    for axis_at, blocks in pieces:
        heights = jax.random.uniform(jax.random.fold_in(jax.random.fold_in(own_key, 6), axis_at), (blocks,), jnp.float32, low / len(pieces), top_value / len(pieces))
        loudness = loudness * jnp.repeat(jnp.exp(heights), shape[axis_at] // blocks).reshape((-1,) + (1,) * (len(shape) - 1 - axis_at))
    return loudness


def routed_block(stream_key, own, number, rows, number_of, top, reach, slope):
    order = jax.random.permutation(stream_key, number_of)
    heavy_load, usual = shares(number_of, rows * top, reach, slope, True), shares(number_of, rows * top, reach, slope, False)
    places = jnp.arange(number_of)

    def named(sizes, rotation):
        used = int((sizes > 0).sum())
        fixed = max(1, used // 4)
        moved = fixed + (places - fixed + rotation * (used - fixed)) % max(1, number_of - fixed)
        return jnp.zeros((number_of,), jnp.int32).at[order[jnp.where(places < fixed, places, moved)]].set(jnp.asarray(sizes, jnp.int32))

    sizes = jnp.where(number % 4 == 0, named(heavy_load, number // 4), named(usual, number - number // 4 - 1))
    mixed = jax.random.permutation(jax.random.fold_in(own, 3), number_of)
    source_of, sink = mixed[0:number_of // 2 * 2:2], mixed[1:number_of // 2 * 2:2]
    margin = jnp.minimum(sizes[source_of] - 1, reach - sizes[sink]) // 2
    margin = jnp.where((source_of == order[0]) | (sink == order[0]) | (sizes[sink] == 0), 0, jnp.maximum(margin, 0))
    moved = jax.random.randint(jax.random.fold_in(own, 4), (number_of // 2,), 0, 1 << 20) % (margin + 1)
    sizes = sizes.at[source_of].add(-moved).at[sink].add(moved)
    items = jnp.searchsorted(jnp.cumsum(sizes), jnp.arange(rows * top), side="right").astype(jnp.int32)
    table = items.reshape(top, rows).T
    table = table[jax.random.permutation(jax.random.fold_in(own, 1), rows)]
    rotation = jax.random.randint(jax.random.fold_in(own, 2), (rows, 1), 0, top)
    return jnp.take_along_axis(table, (jnp.arange(top)[None, :] + rotation) % top, axis=1)


def shares(count, total, reach, skew, full):
    portions = [(1 << 20) // math.isqrt(standing ** skew) + 1 for standing in range(1, count + 1)]
    largest = reach if full else min(reach, max(-(-total // count), total * portions[0] // sum(portions)))
    least = 1 if total - largest >= count - 1 else 0
    holding, rest = [largest] + [least] * (count - 1), total - largest - least * (count - 1)
    while rest > 0:
        candidates = [i for i in range(1, count) if holding[i] < largest] or [i for i in range(1, count) if holding[i] < reach]
        whole, budget = sum([portions[i] for i in candidates]), rest
        for i in candidates:
            addition = min(reach - holding[i], max(1, budget * portions[i] // whole), rest)
            holding[i] = holding[i] + addition
            rest = rest - addition
    return np.array(holding)


def normal_values(rng, dims, scale, most, cuts=(), held_as=jnp.bfloat16):
    array = scale * jax.random.normal(rng, dims, jnp.float32)
    if cuts:
        array = array * levels(rng, dims, cuts, -0.22, 0.18)
    return jnp.clip(array, -most, most).astype(held_as)


def setup_inputs(seed: int = 0) -> dict:
    key_of = jax.random.split(jax.random.key(seed), 15)
    patches = normal_values(key_of[0], (LAT, LON, D), 1.0, 6.0, ((0, 8), (1, 32)))
    patch_mask = set_ends((jax.random.randint(key_of[1], (LAT, LON), 0, 5) < 3).astype(jnp.int32), jax.random.fold_in(key_of[1], 1), 0, 1)
    mask_token = normal_values(key_of[2], (D,), 1.0, 6.0)
    w_qkv = normal_values(key_of[3], (D, 3 * D), D ** -0.5, 0.25)
    w_proj = normal_values(key_of[4], (D, D), D ** -0.5, 0.25)
    logit_scale = jnp.clip(jnp.exp(jax.random.uniform(key_of[5], (HEADS,), jnp.float32, math.log(2.0), math.log(20.0))), 2.0, 20.0)
    rel_bias = normal_values(key_of[6], (HEADS, WIN * WIN, WIN * WIN), 1.0, 4.0, (), jnp.float32)
    attn_gain = jnp.clip(1.0 + 0.18 * jax.random.normal(key_of[7], (D,), jnp.float32), 0.1, 1.9)
    moe_gain = jnp.clip(1.0 + 0.18 * jax.random.normal(key_of[8], (D,), jnp.float32), 0.1, 1.9)
    router = normal_values(key_of[9], (D, EXPERTS), 0.09, 0.5)
    expert_ids_keys = jax.random.split(jax.random.fold_in(key_of[10], 1), BANDS_LAT * BANDS_LON * TOK_DEV // TOK_DEV)
    expert_ids_turns = jax.random.permutation(jax.random.fold_in(key_of[10], 3), BANDS_LAT * BANDS_LON * TOK_DEV // TOK_DEV)
    expert_ids = jax.vmap(lambda own, number: routed_block(jax.random.fold_in(key_of[10], 2), own, number, TOK_DEV, EXPERTS, 1, CAP, 2))(expert_ids_keys, expert_ids_turns).reshape((BANDS_LAT, BANDS_LON, TOK_DEV, 1))
    w_in = normal_values(key_of[11], (EXPERTS, D, FF), D ** -0.5, 0.25, ((0, 32),))
    w_out = normal_values(key_of[12], (EXPERTS, D, FF), FF ** -0.5, 0.125, ((0, 32),))
    cotangent = normal_values(key_of[13], (LAT, LON, D), 1.0, 6.0, ((0, 8), (1, 32)))
    return dict(patches=patches, patch_mask=patch_mask, mask_token=mask_token, w_qkv=w_qkv, w_proj=w_proj, logit_scale=logit_scale, rel_bias=rel_bias, attn_gain=attn_gain, moe_gain=moe_gain, router=router, expert_ids=expert_ids, w_in=w_in, w_out=w_out, cotangent=cotangent)


def layer_norm(values, gain):
    average = lax.optimization_barrier(jnp.mean(values, axis=-1, keepdims=True))
    centred = values - average
    variance = lax.optimization_barrier(jnp.mean(centred * centred, axis=-1, keepdims=True))
    return centred * lax.rsqrt(variance + 1e-05) * gain

def norm_backward(values, gain, upstream):
    average = lax.optimization_barrier(jnp.mean(values, axis=-1, keepdims=True))
    centred = values - average
    variance = lax.optimization_barrier(jnp.mean(centred * centred, axis=-1, keepdims=True))
    inv_std = lax.rsqrt(variance + 1e-05)
    normal_part = centred * inv_std
    scaled = upstream * gain
    first_mean = lax.optimization_barrier(jnp.mean(scaled, axis=-1, keepdims=True))
    second_mean = lax.optimization_barrier(jnp.mean(scaled * normal_part, axis=-1, keepdims=True))
    return inv_std * (scaled - first_mean - normal_part * second_mean)

def gelu_parts(preact):
    normal_cdf = 0.5 * (1.0 + jax.scipy.special.erf(preact * 0.7071067811865476))
    density = jnp.exp(-0.5 * preact * preact) * 0.3989422804014327
    return (preact * normal_cdf, normal_cdf + preact * density)

def to_windows(block):
    height, lateral, channels = block.shape
    tiled = block.reshape(height // WIN, WIN, lateral // WIN, WIN, channels).transpose(0, 2, 1, 3, 4)
    return tiled.reshape(height // WIN * (lateral // WIN), WIN * WIN, channels)

def from_windows(windows, height, lateral):
    channels = windows.shape[-1]
    block = windows.reshape(height // WIN, lateral // WIN, WIN, WIN, channels).transpose(0, 2, 1, 3, 4)
    return block.reshape(height, lateral, channels)

def window_labels(row_labels, lateral):
    height = row_labels.shape[0]
    grid = jnp.broadcast_to(row_labels.reshape(height // WIN, 1, WIN, 1), (height // WIN, lateral // WIN, WIN, WIN))
    return grid.reshape(height // WIN * (lateral // WIN), WIN * WIN)

def window_attention(windows, labels, w_qkv, w_proj, logit_scale, rel_bias, attn_gain):
    window_count, window_size, channels = windows.shape
    head_count = rel_bias.shape[0]
    flat = windows.reshape(window_count * window_size, channels)
    projected = jnp.dot(flat, w_qkv, preferred_element_type=jnp.float32).astype(jnp.bfloat16)
    projected = projected.reshape(window_count, window_size, 3, head_count, channels // head_count).astype(jnp.float32)
    queries = projected[:, :, 0]
    key_vecs = projected[:, :, 1]
    value_vecs = projected[:, :, 2]
    queries = queries * lax.rsqrt(lax.optimization_barrier(jnp.sum(queries * queries, axis=-1, keepdims=True)) + 1e-06)
    key_vecs = key_vecs * lax.rsqrt(lax.optimization_barrier(jnp.sum(key_vecs * key_vecs, axis=-1, keepdims=True)) + 1e-06)
    scores = jnp.einsum('wqhc,wkhc->whqk', queries, key_vecs) * logit_scale[None, :, None, None] + rel_bias[None]
    allowed = (labels[:, :, None] == labels[:, None, :])[:, None]
    weights = jnp.where(allowed, jnp.exp(scores), 0.0)
    weights = (weights / lax.optimization_barrier(jnp.sum(weights, axis=-1, keepdims=True))).astype(jnp.bfloat16)
    blended = jnp.einsum('whqk,wkhc->wqhc', weights.astype(jnp.float32), value_vecs).astype(jnp.bfloat16)
    projection = jnp.dot(blended.reshape(window_count * window_size, channels), w_proj, preferred_element_type=jnp.float32)
    resid = flat.astype(jnp.float32) + layer_norm(projection, attn_gain)
    return resid.astype(jnp.bfloat16).reshape(window_count, window_size, channels)

def reference(patches, patch_mask, mask_token, w_qkv, w_proj, logit_scale, rel_bias, attn_gain, moe_gain, router, expert_ids, w_in, w_out, cotangent):
    masked = jnp.where(patch_mask[:, :, None] == 1, mask_token[None, None, :], patches)
    displaced = jnp.roll(masked, (-SHIFT, -SHIFT), axis=(0, 1))
    grid_rows = jnp.arange(LAT, dtype=jnp.int32)
    row_labels = (grid_rows >= LAT - SHIFT).astype(jnp.int32)

    def attend_band(pair):
        block, labels = pair
        result = window_attention(to_windows(block), window_labels(labels, LON), w_qkv, w_proj, logit_scale, rel_bias, attn_gain)
        return from_windows(result, WIN, LON)
    hidden = lax.map(attend_band, (displaced.reshape(LAT // WIN, WIN, LON, D), row_labels.reshape(LAT // WIN, WIN)))
    hidden = hidden.reshape(LAT, LON, D)

    def per_device(grid):
        return grid.reshape(N_LAT, HL, N_LON, WL, D).transpose(0, 2, 1, 3, 4).reshape(N_LAT, N_LON, TOK_DEV, D)
    hidden_dev = per_device(hidden)
    cot_dev = per_device(cotangent)
    hidden_f = hidden_dev.astype(jnp.float32)
    normed = layer_norm(hidden_f, moe_gain).astype(jnp.bfloat16)
    logits = jnp.dot(normed.reshape(-1, D), router, preferred_element_type=jnp.float32).reshape(N_LAT, N_LON, TOK_DEV, EXPERTS)
    chosen_ids = expert_ids[..., 0]
    onehot = (chosen_ids[..., None] == jnp.arange(EXPERTS, dtype=jnp.int32)).astype(jnp.float32)
    gate = jax.nn.sigmoid(lax.optimization_barrier(jnp.sum(logits * onehot, axis=-1)))
    scaled_cot = (gate[..., None] * cot_dev.astype(jnp.float32)).astype(jnp.bfloat16)
    slots = lax.optimization_barrier(jnp.sum((jnp.cumsum(onehot, axis=2) - onehot) * onehot, axis=-1)).astype(jnp.int32)
    band_index = jnp.broadcast_to(jnp.arange(N_LAT, dtype=jnp.int32)[:, None, None], chosen_ids.shape)
    lon_index = jnp.broadcast_to(jnp.arange(N_LON, dtype=jnp.int32)[None, :, None], chosen_ids.shape)
    normed_buf = jnp.zeros((N_LAT, EXPERTS, N_LON, CAP, D), jnp.bfloat16).at[band_index, chosen_ids, lon_index, slots].set(normed)
    cot_buf = jnp.zeros((N_LAT, EXPERTS, N_LON, CAP, D), jnp.bfloat16).at[band_index, chosen_ids, lon_index, slots].set(scaled_cot)

    def expert_pass(inputs):
        weight_in, weight_out, normed_slots, cot_slots = inputs

        def band_step(totals, pair):
            z_slots = pair[0].reshape(N_LON * CAP, D)
            d_slots = pair[1].reshape(N_LON * CAP, D)
            preact = jnp.dot(z_slots, weight_in, preferred_element_type=jnp.float32)
            activation, slopes = gelu_parts(preact)
            activation = activation.astype(jnp.bfloat16)
            outputs = jnp.dot(activation, weight_out.T, preferred_element_type=jnp.float32).astype(jnp.bfloat16)
            dact = jnp.dot(d_slots, weight_out, preferred_element_type=jnp.float32)
            dpreact = (dact * slopes).astype(jnp.bfloat16)
            dnormed_slots = jnp.dot(dpreact, weight_in.T, preferred_element_type=jnp.float32).astype(jnp.bfloat16)
            grad_in = jnp.dot(z_slots.T, dpreact, preferred_element_type=jnp.float32).astype(jnp.bfloat16)
            grad_out = jnp.dot(d_slots.T, activation, preferred_element_type=jnp.float32).astype(jnp.bfloat16)
            grad_in, grad_out = lax.optimization_barrier((grad_in, grad_out))
            partial_grads = jnp.concatenate([grad_in.astype(jnp.float32), grad_out.astype(jnp.float32)], axis=1)
            return (totals + partial_grads, (outputs.reshape(N_LON, CAP, D), dnormed_slots.reshape(N_LON, CAP, D)))
        totals, (outputs, dnormed_slots) = lax.scan(band_step, jnp.zeros((D, 2 * FF), jnp.float32), (normed_slots, cot_slots))
        return (totals, outputs, dnormed_slots)
    grads, expert_outs, dnormed_bufs = lax.map(expert_pass, (w_in, w_out, jnp.moveaxis(normed_buf, 1, 0), jnp.moveaxis(cot_buf, 1, 0)))
    expert_out = expert_outs[chosen_ids, band_index, lon_index, slots]
    dnormed_exp = dnormed_bufs[chosen_ids, band_index, lon_index, slots]
    block_dev = (hidden_f + gate[..., None] * expert_out.astype(jnp.float32)).astype(jnp.bfloat16)
    cot_f = cot_dev.astype(jnp.float32)
    dgate = lax.optimization_barrier(jnp.sum(cot_f * expert_out.astype(jnp.float32), axis=-1))
    dlogit = dgate * gate * (1.0 - gate)
    coeffs = (dlogit[..., None] * onehot).reshape(-1, EXPERTS)
    router_part = jnp.dot(coeffs, router.astype(jnp.float32).T, precision=lax.Precision.HIGHEST).reshape(N_LAT, N_LON, TOK_DEV, D)
    dnormed = dnormed_exp.astype(jnp.float32) + router_part
    grad_dev = cot_f + norm_backward(hidden_f, moe_gain, dnormed)

    def to_grid(values):
        return values.reshape(N_LAT, N_LON, HL, WL, D).transpose(0, 2, 1, 3, 4).reshape(LAT, LON, D)
    weight_grads = jnp.transpose(grads, (1, 0, 2))
    return (to_grid(block_dev), to_grid(grad_dev), weight_grads)
```

```python
import jax
import jax.numpy as jnp
from jax import lax
from jax.experimental import pallas as pl
from jax.experimental.pallas import tpu as pltpu
from jax.sharding import PartitionSpec as P

WIN = 8
SHIFT = 4
BF16 = jnp.bfloat16
F32 = jnp.float32
I32 = jnp.int32
VMEM_BYTES = 48 * 1024 * 1024


def call(body, outs, *operands, scratch=(), smem=()):
    specs = [
        pl.BlockSpec(memory_space=pltpu.SMEM if i in smem else pltpu.VMEM)
        for i in range(len(operands))
    ]
    return pl.pallas_call(
        body,
        out_shape=outs,
        in_specs=specs,
        out_specs=jax.tree.map(lambda _: pl.BlockSpec(memory_space=pltpu.VMEM), outs),
        scratch_shapes=list(scratch),
        compiler_params=pltpu.CompilerParams(vmem_limit_bytes=VMEM_BYTES),
    )(*operands)


def shape(dims, dtype):
    return jax.ShapeDtypeStruct(dims, dtype)


def dot(a, b):
    return jnp.dot(a, b, preferred_element_type=F32)


def dot_nt(a, b):
    return lax.dot_general(a, b, (((1,), (1,)), ((), ())), preferred_element_type=F32)


def dot_tn(a, b):
    return lax.dot_general(a, b, (((0,), (0,)), ((), ())), preferred_element_type=F32)


def halves(values):
    high = values.astype(BF16)
    return high, (values - high.astype(F32)).astype(BF16)


def dot_split(values, ones):
    high, low = halves(values)
    return dot(high, ones) + dot(low, ones)


def iota(dims, axis):
    return lax.broadcasted_iota(I32, dims, axis)


def flag(condition):
    return jnp.where(condition, 1.0, 0.0).astype(BF16)


def normal_form(values):
    centred = values - jnp.mean(values, axis=-1, keepdims=True)
    inv_std = lax.rsqrt(jnp.mean(centred * centred, axis=-1, keepdims=True) + 1e-05)
    return centred * inv_std, inv_std


def gelu_parts(preact):
    normal_cdf = 0.5 * (1.0 + lax.erf(preact * 0.7071067811865476))
    density = jnp.exp(-0.5 * preact * preact) * 0.3989422804014327
    return preact * normal_cdf, normal_cdf + preact * density


def passed_along(block, axis, distance):
    devices = range(lax.axis_size(axis))
    route = [((i - distance) % len(devices), i) for i in devices]
    return lax.ppermute(block, axis, route)


def passed_diagonally(block):
    rows, columns = lax.axis_size("lat"), lax.axis_size("lon")
    route = [
        ((i + 1) % rows * columns + (j + 1) % columns, i * columns + j)
        for i in range(rows)
        for j in range(columns)
    ]
    return lax.ppermute(block, ("lat", "lon"), route)


def exchanged(slots):
    return lax.all_to_all(slots, "lon", split_axis=0, concat_axis=0, tiled=True)


def slot_kernel(expert_total, capacity, ids_ref, cot_ref, send_ref, row_ref, col_ref):
    tokens = cot_ref.shape[0]
    ids = ids_ref[...]
    onehot = iota((expert_total, tokens), 0) == ids
    before = flag(iota((tokens, tokens), 0) < iota((tokens, tokens), 1))
    earlier = dot(flag(onehot), before)
    slot = jnp.sum(jnp.where(onehot, earlier, 0.0), axis=0, keepdims=True).astype(I32)
    target = ids * capacity + slot
    row_ref[...] = target
    diagonal = iota((tokens, tokens), 0) == iota((tokens, tokens), 1)
    column = jnp.sum(jnp.where(diagonal, target, 0).astype(F32), axis=1, keepdims=True)
    col_ref[...] = jnp.broadcast_to(column.astype(I32), col_ref.shape)
    placed = flag(iota((send_ref.shape[0], tokens), 0) == target)
    send_ref[...] = dot(placed, cot_ref[...]).astype(BF16)


def attention_kernel(
    heads,
    flag_ref,
    patches_ref,
    mask_ref,
    token_ref,
    right_ref,
    low_ref,
    corner_ref,
    qkv_ref,
    proj_ref,
    scale_ref,
    bias_ref,
    attn_gain_ref,
    moe_gain_ref,
    router_ref,
    row_ref,
    col_ref,
    hidden_ref,
    send_ref,
    gate_ref,
    blended_ref,
):
    tokens, width = patches_ref.shape
    height, lateral = mask_ref.shape
    features = width // heads
    window = WIN * WIN
    across = lateral // WIN
    group = 128 // features
    expert_total = router_ref.shape[0]
    capacity = send_ref.shape[0] // expert_total

    in_row = flag(iota((tokens, height), 0) // lateral == iota((tokens, height), 1))
    spread = dot(in_row, mask_ref[...].astype(F32).astype(BF16))
    own = iota((tokens, lateral), 0) % lateral == iota((tokens, lateral), 1)
    hidden_patch = jnp.sum(jnp.where(own, spread, 0.0), axis=1, keepdims=True)
    masked = jnp.where(
        hidden_patch > 0.5, token_ref[...].astype(F32), patches_ref[...].astype(F32)
    ).astype(BF16)
    source = jnp.concatenate([masked, right_ref[...], low_ref[...], corner_ref[...]], axis=0)

    place = iota((tokens, 1), 0)
    which, inside = place // window, place % window
    row = which // across * WIN + inside // WIN + SHIFT
    column = which % across * WIN + inside % WIN + SHIFT
    right_base = tokens
    low_base = right_base + height * SHIFT
    corner_base = low_base + SHIFT * lateral
    local = row * lateral + column
    from_right = right_base + row * SHIFT + column - lateral
    from_low = low_base + (row - height) * lateral + column
    from_corner = corner_base + (row - height) * SHIFT + column - lateral
    origin = jnp.where(
        row < height,
        jnp.where(column < lateral, local, from_right),
        jnp.where(column < lateral, from_low, from_corner),
    )
    moves = flag(iota((tokens, source.shape[0]), 1) == origin)
    displaced_f = dot(moves, source)
    displaced = displaced_f.astype(BF16)

    projected = dot(displaced, qkv_ref[...]).astype(BF16)
    head_of = flag(iota((width, heads), 0) // features == iota((width, heads), 1))
    of_head = flag(iota((heads, width), 1) // features == iota((heads, width), 0))
    queries = projected[:, :width].astype(F32)
    keys = projected[:, width : 2 * width].astype(F32)
    query_norm = lax.rsqrt(dot_split(queries * queries, head_of) + 1e-06) * scale_ref[...]
    key_norm = lax.rsqrt(dot_split(keys * keys, head_of) + 1e-06)
    queries = (queries * dot_split(query_norm, of_head)).astype(BF16)
    keys = (keys * dot_split(key_norm, of_head)).astype(BF16)

    block = group * window
    member = flag(
        iota((block, 128), 0) // window == iota((block, 128), 1) // features
    )
    split = (iota((window, block), 0) >= window // 2) == (
        iota((window, block), 1) % window >= window // 2
    )
    allowed = jnp.where(split, 1.0, jnp.where(flag_ref[0] == 1, 0.0, 1.0))
    for w in range(tokens // window):
        rows = slice(w * window, (w + 1) * window)
        for g in range(width // 128):
            lanes = slice(g * 128, (g + 1) * 128)
            q = queries[rows, lanes]
            k = keys[rows, lanes]
            v = projected[rows, 2 * width + g * 128 : 2 * width + (g + 1) * 128]
            wide_k = jnp.concatenate([k] * group, axis=0) * member
            wide_v = jnp.concatenate([v] * group, axis=0) * member
            scores = dot_nt(q, wide_k) + bias_ref[:, g * block : (g + 1) * block]
            weights = jnp.exp(scores)
            if w >= across * (height // WIN - 1):
                weights = weights * allowed
            both = dot(weights.astype(BF16), jnp.concatenate([wide_v, member], axis=1))
            blended_ref[rows, lanes] = (both[:, :128] / both[:, 128:]).astype(BF16)

    projection = dot(blended_ref[...], proj_ref[...])
    branch, _ = normal_form(projection)
    hidden = displaced_f + branch * attn_gain_ref[...]
    hidden = hidden.reshape(height // WIN, across, WIN, WIN, width).transpose(0, 2, 1, 3, 4)
    hidden = hidden.reshape(tokens, width).astype(BF16)
    hidden_ref[...] = hidden
    normed, _ = normal_form(hidden.astype(F32))
    normed = (normed * moe_gain_ref[...]).astype(BF16)
    logits = dot_nt(normed, router_ref[...])
    chosen = iota((tokens, expert_total), 1) == col_ref[:, :1] // capacity
    gate = jax.nn.sigmoid(jnp.sum(jnp.where(chosen, logits, 0.0), axis=1, keepdims=True))
    gate_ref[...] = jnp.broadcast_to(gate, gate_ref.shape)
    placed = flag(iota((send_ref.shape[0], tokens), 0) == row_ref[...])
    send_ref[...] = dot(placed, normed).astype(BF16)


CHUNK = 512


def early_kernel(d_ref, w_out_ref, dact_ref):
    for start in range(0, w_out_ref.shape[1], CHUNK):
        part = slice(start, start + CHUNK)
        dact_ref[:, part] = dot(d_ref[...], w_out_ref[:, part])


def forward_kernel(index_ref, z_ref, w_in_ref, w_out_ref, router_ref, out_ref, act_ref, slope_ref, gate_ref):
    z = z_ref[...]
    total = None
    for start in range(0, w_in_ref.shape[1], CHUNK):
        part = slice(start, start + CHUNK)
        activation, slopes = gelu_parts(dot(z, w_in_ref[:, part]))
        activation = activation.astype(BF16)
        act_ref[:, part] = activation
        slope_ref[:, part] = slopes
        piece = dot_nt(activation, w_out_ref[:, part])
        total = piece if total is None else total + piece
    out_ref[...] = total.astype(BF16)
    logits = dot_nt(z, router_ref[...])
    mine = iota(logits.shape, 1) == index_ref[0]
    gate = jax.nn.sigmoid(jnp.sum(jnp.where(mine, logits, 0.0), axis=1, keepdims=True))
    gate_ref[...] = jnp.broadcast_to(gate, gate_ref.shape)


def backward_kernel(gate_ref, d_ref, dact_ref, slope_ref, w_in_ref, back_ref, dpre_ref, scaled_ref):
    gate = gate_ref[:, :1]
    scaled_ref[...] = (d_ref[...].astype(F32) * gate).astype(BF16)
    total = None
    for start in range(0, w_in_ref.shape[1], CHUNK):
        part = slice(start, start + CHUNK)
        dpre = (dact_ref[:, part] * gate * slope_ref[:, part]).astype(BF16)
        dpre_ref[:, part] = dpre
        piece = dot_nt(dpre, w_in_ref[:, part])
        total = piece if total is None else total + piece
    back_ref[...] = total.astype(BF16)


def grads_kernel(z_ref, dpre_ref, d_ref, act_ref, grad_ref):
    hidden_units = dpre_ref.shape[1]
    for start in range(0, hidden_units, CHUNK):
        part = slice(start, start + CHUNK)
        grad_ref[:, part] = dot_tn(z_ref[...], dpre_ref[:, part]).astype(BF16)
    for start in range(0, hidden_units, CHUNK):
        part = slice(start, start + CHUNK)
        later = slice(hidden_units + start, hidden_units + start + CHUNK)
        grad_ref[:, later] = dot_tn(d_ref[...], act_ref[:, part]).astype(BF16)


def picked(col_ref, slots_ref):
    tokens, total = col_ref.shape[0], slots_ref.shape[0]
    picks = flag(iota((tokens, total), 1) == col_ref[:, :1])
    return dot(picks, slots_ref[...])


def output_kernel(col_ref, back_ref, hidden_ref, gate_ref, cot_ref, block_ref, dlogit_ref):
    expert_out = picked(col_ref, back_ref)
    gate = gate_ref[:, :1]
    block_ref[...] = (hidden_ref[...].astype(F32) + gate * expert_out).astype(BF16)
    dgate = jnp.sum(cot_ref[...].astype(F32) * expert_out, axis=1, keepdims=True)
    dlogit_ref[...] = jnp.broadcast_to(dgate * gate * (1.0 - gate), dlogit_ref.shape)


def mixer_kernel(
    capacity, col_ref, back_ref, hidden_ref, dlogit_ref, cot_ref, router_ref, gain_ref, mixer_ref
):
    tokens = col_ref.shape[0]
    dnormed = picked(col_ref, back_ref)
    chosen = iota((tokens, router_ref.shape[0]), 1) == col_ref[:, :1] // capacity
    dnormed = dnormed + dlogit_ref[:, :1] * dot(flag(chosen), router_ref[...])
    xhat, inv_std = normal_form(hidden_ref[...].astype(F32))
    scaled = dnormed * gain_ref[...]
    first = jnp.mean(scaled, axis=-1, keepdims=True)
    second = jnp.mean(scaled * xhat, axis=-1, keepdims=True)
    mixer_ref[...] = cot_ref[...].astype(F32) + inv_std * (scaled - first - xhat * second)


def per_device(
    patches,
    patch_mask,
    mask_token,
    w_qkv,
    w_proj,
    logit_scale,
    rel_bias,
    attn_gain,
    moe_gain,
    router,
    expert_ids,
    w_in,
    w_out,
    cotangent,
):
    height, lateral, width = patches.shape
    tokens = height * lateral
    heads, window, _ = rel_bias.shape
    expert_total = router.shape[1]
    capacity = 2 * tokens // expert_total
    slot_total = expert_total * capacity
    w_in, w_out = w_in[0], w_out[0]
    units = w_in.shape[1]

    def rim(rows, columns):
        return jnp.where(
            patch_mask[rows, columns, None] == 1, mask_token[None, None, :], patches[rows, columns]
        )

    few, whole = slice(0, SHIFT), slice(None)
    right = passed_along(rim(whole, few).reshape(height * SHIFT, width), "lon", -1)
    low = passed_along(rim(few, whole).reshape(SHIFT * lateral, width), "lat", -1)
    corner = passed_diagonally(rim(few, few).reshape(SHIFT * SHIFT, width))

    cot = cotangent.reshape(tokens, width)
    router_t = router.T
    cot_send, target_row, target_col = call(
        lambda *refs: slot_kernel(expert_total, capacity, *refs),
        (
            shape((slot_total, width), BF16),
            shape((1, tokens), I32),
            shape((tokens, 128), I32),
        ),
        expert_ids.reshape(1, tokens),
        cot,
    )
    d_slots = exchanged(cot_send.reshape(expert_total, capacity, width)).reshape(slot_total, width)

    last = (lax.axis_index("lat") == lax.axis_size("lat") - 1).astype(I32).reshape(1)
    bias = rel_bias.transpose(1, 0, 2).reshape(window, heads * window)
    hidden, normed_send, gate = call(
        lambda *refs: attention_kernel(heads, *refs),
        (
            shape((tokens, width), BF16),
            shape((slot_total, width), BF16),
            shape((tokens, 128), F32),
        ),
        last,
        patches.reshape(tokens, width),
        patch_mask,
        mask_token.reshape(1, width),
        right,
        low,
        corner,
        w_qkv,
        w_proj,
        logit_scale.reshape(1, heads),
        bias,
        attn_gain.reshape(1, width),
        moe_gain.reshape(1, width),
        router_t,
        target_row,
        target_col,
        scratch=[pltpu.VMEM((tokens, width), BF16)],
        smem=(0,),
    )
    z_slots = exchanged(normed_send.reshape(expert_total, capacity, width)).reshape(
        slot_total, width
    )
    dact = call(early_kernel, shape((slot_total, units), F32), d_slots, w_out)
    outputs, activation, slopes, slot_gate = call(
        forward_kernel,
        (
            shape((slot_total, width), BF16),
            shape((slot_total, units), BF16),
            shape((slot_total, units), F32),
            shape((slot_total, 128), F32),
        ),
        lax.axis_index("lon").astype(I32).reshape(1),
        z_slots,
        w_in,
        w_out,
        router_t,
        smem=(0,),
    )
    out_back = exchanged(outputs.reshape(expert_total, capacity, width)).reshape(slot_total, width)
    dnormed, dpre, scaled = call(
        backward_kernel,
        (
            shape((slot_total, width), BF16),
            shape((slot_total, units), BF16),
            shape((slot_total, width), BF16),
        ),
        slot_gate,
        d_slots,
        dact,
        slopes,
        w_in,
    )
    dnormed_back = exchanged(dnormed.reshape(expert_total, capacity, width)).reshape(
        slot_total, width
    )
    grads = call(grads_kernel, shape((width, 2 * units), BF16), z_slots, dpre, scaled, activation)
    weight_grads = lax.psum_scatter(grads, "lat", scatter_dimension=0, tiled=True).astype(F32)
    block_out, dlogit = call(
        output_kernel,
        (shape((tokens, width), BF16), shape((tokens, 128), F32)),
        target_col,
        out_back,
        hidden,
        gate,
        cot,
    )
    mixer_grad = call(
        lambda *refs: mixer_kernel(capacity, *refs),
        shape((tokens, width), F32),
        target_col,
        dnormed_back,
        hidden,
        dlogit,
        cot,
        router_t,
        moe_gain.reshape(1, width),
    )
    return (
        block_out.reshape(height, lateral, width),
        mixer_grad.reshape(height, lateral, width),
        weight_grads.reshape(-1, 1, 2 * units),
    )


def solution(mesh):
    placed = (
        P("lat", "lon", None),
        P("lat", "lon"),
        P(),
        P(),
        P(),
        P(),
        P(),
        P(),
        P(),
        P(),
        P("lat", "lon", None, None),
        P("lon", None, None),
        P("lon", None, None),
        P("lat", "lon", None),
    )
    return jax.shard_map(
        per_device,
        mesh=mesh,
        in_specs=placed,
        out_specs=(P("lat", "lon", None), P("lat", "lon", None), P("lat", "lon", None)),
        check_vma=False,
    )
```

```python
import math

import jax
import jax.numpy as jnp
from jax import lax
from jax.experimental import pallas as pl
from jax.experimental.pallas import tpu as pltpu
from jax.sharding import PartitionSpec as P

WIN = 8
SHIFT = 4
BF16 = jnp.bfloat16
F32 = jnp.float32
I32 = jnp.int32


MIB = 1024 * 1024
WHOLE = pl.BlockSpec(memory_space=pltpu.VMEM)
SCALAR = pl.BlockSpec(memory_space=pltpu.SMEM)
FAR = pl.BlockSpec(memory_space=pltpu.HBM)
UNREAD = pl.BlockSpec(memory_space=pl.ANY)


def call(body, outs, ins, *operands, scratch=(), grid=(), out_specs=None, vmem=16, flops=0):
    if out_specs is None:
        out_specs = jax.tree.map(lambda _: WHOLE, outs)
    moved = sum(math.prod(x.shape) * x.dtype.itemsize for x in (*operands, *jax.tree.leaves(outs)))
    return pl.pallas_call(
        body,
        grid=grid,
        out_shape=outs,
        in_specs=list(ins),
        out_specs=out_specs,
        scratch_shapes=list(scratch),
        cost_estimate=pl.CostEstimate(
            flops=int(flops), transcendentals=0, bytes_accessed=int(moved)
        ),
        compiler_params=pltpu.CompilerParams(vmem_limit_bytes=vmem * MIB),
    )(*operands)


def shape(dims, dtype):
    return jax.ShapeDtypeStruct(dims, dtype)


def far(dims, dtype):
    return pltpu.HBM(dims, dtype)


def kept_far(array):
    return pltpu.with_memory_space_constraint(array, pltpu.HBM)


def slot_gates(slots, router_t, index):
    logits = dot_nt(slots, router_t)
    mine = iota(logits.shape, 1) == index
    return jax.nn.sigmoid(jnp.sum(jnp.where(mine, logits, 0.0), axis=1, keepdims=True))


def dot(a, b):
    return jnp.dot(a, b, preferred_element_type=F32)


def dot_nt(a, b):
    return lax.dot_general(a, b, (((1,), (1,)), ((), ())), preferred_element_type=F32)


def dot_tn(a, b):
    return lax.dot_general(a, b, (((0,), (0,)), ((), ())), preferred_element_type=F32)


def halves(values):
    high = values.astype(BF16)
    return high, (values - high.astype(F32)).astype(BF16)


def dot_split(values, ones):
    high, low = halves(values)
    return dot(high, ones) + dot(low, ones)


def iota(dims, axis):
    return lax.broadcasted_iota(I32, dims, axis)


def flag(condition):
    return jnp.where(condition, 1.0, 0.0).astype(BF16)


def normal_form(values):
    centred = values - jnp.mean(values, axis=-1, keepdims=True)
    inv_std = lax.rsqrt(jnp.mean(centred * centred, axis=-1, keepdims=True) + 1e-05)
    return centred * inv_std, inv_std


def doubled_gelu_parts(preact):
    scaled = preact * 0.7071067811865476
    doubled_cdf = 1.0 + lax.erf(scaled)
    bell = jnp.exp(-(scaled * scaled))
    return preact * doubled_cdf, doubled_cdf + preact * 0.7978845608028654 * bell


def passed_along(block, axis, distance):
    devices = range(lax.axis_size(axis))
    route = [((i - distance) % len(devices), i) for i in devices]
    return lax.ppermute(block, axis, route)


def passed_diagonally(block):
    rows, columns = lax.axis_size("lat"), lax.axis_size("lon")
    route = [
        ((i + 1) % rows * columns + (j + 1) % columns, i * columns + j)
        for i in range(rows)
        for j in range(columns)
    ]
    return lax.ppermute(block, ("lat", "lon"), route)


def exchanged(slots):
    return lax.all_to_all(slots, "lon", split_axis=0, concat_axis=0, tiled=True)


def send_rows(placed_rows, rows, staged_ref, out_ref, sems):
    copies = []
    for i in range(sems.shape[0]):
        step = out_ref.shape[0] // sems.shape[0]
        part = slice(i * step, (i + 1) * step)
        staged_ref[part] = dot(placed_rows(i * step, step), rows).astype(BF16)
        copies.append(pltpu.make_async_copy(staged_ref.at[part], out_ref.at[part], sems.at[i]))
        copies[-1].start()
    return copies


def slot_kernel(
    expert_total,
    capacity,
    masked_ref,
    ids_ref,
    cot_ref,
    send_ref,
    row_ref,
    col_ref,
    cots,
    staged,
    sem,
    sems,
):
    del masked_ref
    load = pltpu.make_async_copy(cot_ref, cots, sem.at[0])
    load.start()
    tokens = cot_ref.shape[0]
    ids = ids_ref[...]
    onehot = iota((expert_total, tokens), 0) == ids
    before = flag(iota((tokens, tokens), 0) < iota((tokens, tokens), 1))
    earlier = dot(flag(onehot), before)
    slot = jnp.sum(jnp.where(onehot, earlier, 0.0), axis=0, keepdims=True).astype(I32)
    target = ids * capacity + slot
    load.wait()
    copies = send_rows(
        lambda start, step: flag(iota((step, tokens), 0) + start == target),
        cots[...],
        staged,
        send_ref,
        sems,
    )
    row_ref[...] = target
    diagonal = iota((tokens, tokens), 0) == iota((tokens, tokens), 1)
    column = jnp.sum(jnp.where(diagonal, target, 0).astype(F32), axis=1, keepdims=True)
    col_ref[...] = jnp.broadcast_to(column.astype(I32), col_ref.shape)
    for copy in copies:
        copy.wait()


def mask_kernel(patches_ref, mask_ref, token_ref, masked_ref, right_ref, low_ref, corner_ref):
    tokens = patches_ref.shape[0]
    height, lateral = mask_ref.shape
    in_row = flag(iota((tokens, height), 0) // lateral == iota((tokens, height), 1))
    spread = dot(in_row, mask_ref[...].astype(F32).astype(BF16))
    own = iota((tokens, lateral), 0) % lateral == iota((tokens, lateral), 1)
    hidden_patch = jnp.sum(jnp.where(own, spread, 0.0), axis=1, keepdims=True)
    masked = jnp.where(
        hidden_patch > 0.5, token_ref[...].astype(F32), patches_ref[...].astype(F32)
    ).astype(BF16)
    masked_ref[...] = masked
    low_ref[...] = masked[: SHIFT * lateral]
    place = iota((height * SHIFT, tokens), 0)
    picks = flag(place // SHIFT * lateral + place % SHIFT == iota((height * SHIFT, tokens), 1))
    right = dot(picks, masked).astype(BF16)
    right_ref[...] = right
    corner_ref[...] = right[: SHIFT * SHIFT]


def attention_kernel(
    heads,
    height,
    lateral,
    flag_ref,
    masked_ref,
    right_ref,
    low_ref,
    corner_ref,
    qkv_ref,
    proj_ref,
    scale_ref,
    bias_ref,
    attn_gain_ref,
    moe_gain_ref,
    router_ref,
    row_ref,
    col_ref,
    hidden_ref,
    send_ref,
    gate_ref,
    blended_ref,
    staged,
    sems,
):
    tokens, width = masked_ref.shape
    features = width // heads
    window = WIN * WIN
    across = lateral // WIN
    group = 128 // features
    expert_total = router_ref.shape[0]
    capacity = send_ref.shape[0] // expert_total

    source = jnp.concatenate([masked_ref[...], right_ref[...], low_ref[...], corner_ref[...]], axis=0)

    place = iota((tokens, 1), 0)
    which, inside = place // window, place % window
    row = which // across * WIN + inside // WIN + SHIFT
    column = which % across * WIN + inside % WIN + SHIFT
    right_base = tokens
    low_base = right_base + height * SHIFT
    corner_base = low_base + SHIFT * lateral
    local = row * lateral + column
    from_right = right_base + row * SHIFT + column - lateral
    from_low = low_base + (row - height) * lateral + column
    from_corner = corner_base + (row - height) * SHIFT + column - lateral
    origin = jnp.where(
        row < height,
        jnp.where(column < lateral, local, from_right),
        jnp.where(column < lateral, from_low, from_corner),
    )
    moves = flag(iota((tokens, source.shape[0]), 1) == origin)
    displaced_f = dot(moves, source)
    displaced = displaced_f.astype(BF16)

    projected = dot(displaced, qkv_ref[...]).astype(BF16)
    head_of = flag(iota((width, heads), 0) // features == iota((width, heads), 1))
    of_head = flag(iota((heads, width), 1) // features == iota((heads, width), 0))
    queries = projected[:, :width].astype(F32)
    keys = projected[:, width : 2 * width].astype(F32)
    query_norm = lax.rsqrt(dot_split(queries * queries, head_of) + 1e-06) * scale_ref[...]
    key_norm = lax.rsqrt(dot_split(keys * keys, head_of) + 1e-06)
    queries = (queries * dot_split(query_norm, of_head)).astype(BF16)
    keys = (keys * dot_split(key_norm, of_head)).astype(BF16)

    block = group * window
    biases = [
        jnp.concatenate([bias_ref[g * group + i] for i in range(group)], axis=1)
        for g in range(width // 128)
    ]
    member = flag(
        iota((block, 128), 0) // window == iota((block, 128), 1) // features
    )
    split = (iota((window, block), 0) >= window // 2) == (
        iota((window, block), 1) % window >= window // 2
    )
    allowed = jnp.where(split, 1.0, jnp.where(flag_ref[0] == 1, 0.0, 1.0))
    for w in range(tokens // window):
        rows = slice(w * window, (w + 1) * window)
        for g in range(width // 128):
            lanes = slice(g * 128, (g + 1) * 128)
            q = queries[rows, lanes]
            k = keys[rows, lanes]
            v = projected[rows, 2 * width + g * 128 : 2 * width + (g + 1) * 128]
            wide_k = jnp.concatenate([k] * group, axis=0) * member
            wide_v = jnp.concatenate([v] * group, axis=0) * member
            scores = dot_nt(q, wide_k) + biases[g]
            weights = jnp.exp(scores)
            if w >= across * (height // WIN - 1):
                weights = weights * allowed
            both = dot(weights.astype(BF16), jnp.concatenate([wide_v, member], axis=1))
            blended_ref[rows, lanes] = (both[:, :128] / both[:, 128:]).astype(BF16)

    projection = dot(blended_ref[...], proj_ref[...])
    branch, _ = normal_form(projection)
    hidden = displaced_f + branch * attn_gain_ref[...]
    hidden = hidden.reshape(height // WIN, across, WIN, WIN, width).transpose(0, 2, 1, 3, 4)
    hidden = hidden.reshape(tokens, width).astype(BF16)
    hidden_ref[...] = hidden
    normed, _ = normal_form(hidden.astype(F32))
    normed = (normed * moe_gain_ref[...]).astype(BF16)
    copies = send_rows(
        lambda start, step: flag(iota((step, tokens), 0) + start == row_ref[...]),
        normed,
        staged,
        send_ref,
        sems,
    )
    logits = dot_nt(normed, router_ref[...])
    chosen = iota((tokens, expert_total), 1) == col_ref[:, :1] // capacity
    gate = jax.nn.sigmoid(jnp.sum(jnp.where(chosen, logits, 0.0), axis=1, keepdims=True))
    gate_ref[...] = jnp.broadcast_to(gate, gate_ref.shape)
    for copy in copies:
        copy.wait()


PARTS = 4


def early_kernel(d_ref, w_out_ref, dact_ref):
    dact_ref[...] = dot(d_ref[...], w_out_ref[...])


def expert_kernel(
    index_ref,
    z_ref,
    router_ref,
    w_in_ref,
    w_out_ref,
    dact_ref,
    back_ref,
    act_ref,
    dpre_ref,
    w_in,
    w_out,
    dact,
    act,
    dpre,
    back,
    load_sems,
    store_sems,
):
    rows, width = z_ref.shape
    units = w_in.shape[1]
    tile, chunk, piece = rows // PARTS, units // PARTS, width // 2

    def load(source, target, i):
        copy = pltpu.make_async_copy(source, target, load_sems.at[i])
        copy.start()
        return copy

    def tiled(i, step):
        return slice(i * step, (i + 1) * step)

    load_in = [
        load(w_in_ref.at[:, tiled(i, chunk)], w_in.at[:, tiled(i, chunk)], i) for i in range(PARTS)
    ]
    load_dact = [load(dact_ref.at[tiled(0, tile)], dact.at[tiled(0, tile)], PARTS)]
    load_out = load(w_out_ref, w_out, 2 * PARTS)
    load_dact += [
        load(dact_ref.at[tiled(i, tile)], dact.at[tiled(i, tile)], PARTS + i)
        for i in range(1, PARTS)
    ]
    half_gate = 0.5 * slot_gates(z_ref[...], router_ref[...], index_ref[0])
    stores = []

    def store(source, target):
        copy = pltpu.make_async_copy(source, target, store_sems.at[len(stores)])
        copy.start()
        stores.append(copy)

    for r in range(PARTS + 1):
        if r < PARTS:
            load_dact[r].wait()
        if r == 1:
            load_out.wait()
        here, last = tiled(r, tile), tiled(r - 1, tile)
        for c in range(PARTS):
            part = tiled(c, chunk)
            if r < PARTS:
                if r == 0:
                    load_in[c].wait()
                activation, slopes = doubled_gelu_parts(dot(z_ref[here], w_in[:, part]))
                act[here, part] = activation.astype(BF16)
                dpre[here, part] = (dact[here, part] * slopes).astype(BF16)
            if r > 0:
                half = tiled(c % 2, piece)
                if c < 2:
                    result = 0.5 * dot_nt(act[last], w_out[half])
                else:
                    result = half_gate[last] * dot_nt(dpre[last], w_in[half])
                back[last, tiled(c, piece)] = result.astype(BF16)
        if r < PARTS:
            store(act.at[here], act_ref.at[here])
            store(dpre.at[here], dpre_ref.at[here])
        if r > 0:
            store(back.at[last], back_ref.at[last])
    for copy in stores:
        copy.wait()


def grads_kernel(
    lat_total, index_ref, z_ref, d_ref, router_ref, dpre_ref, act_ref, keep_ref, give_ref, zt, dt
):
    width = z_ref.shape[1]
    rows = width // lat_total

    @pl.when(pl.program_id(0) == 0)
    def _():
        place = iota((width, 1), 0)
        half, step, inside = place // (width // 2), place % (width // 2) // rows, place % rows
        column, core = index_ref[1] // 2, index_ref[1] % 2
        block = (step + column) % (lat_total // 2) * 2 + (half + core) % 2
        moves = flag(iota((width, width), 1) == block * rows + inside)
        half_gate = 0.5 * slot_gates(z_ref[...], router_ref[...], index_ref[0])
        for slots_ref, turned in ((z_ref, zt), (d_ref, dt)):
            scaled = (slots_ref[...].astype(F32) * half_gate).astype(BF16)
            turned[...] = dot_nt(moves, scaled).astype(BF16)

    for i, (left, right) in enumerate(((zt, dpre_ref), (dt, act_ref))):
        total = dot(left[...], right[...]).astype(BF16)
        keep_ref[i] = total[: width // 2]
        give_ref[i] = total[width // 2 :]


def pair_kernel(keep_ref, given_ref, own_ref, up_ref, down_ref, up_part_ref, down_part_ref):
    rows = own_ref.shape[1]

    def total(i, step):
        part = slice(step * rows, (step + 1) * rows)
        return (keep_ref[i, part].astype(F32) + given_ref[i, part].astype(F32)).astype(BF16)

    for i in range(2):
        own_ref[i] = total(i, 0)
        up_ref[i] = total(i, 1)
        down_ref[i] = total(i, 3)
    up_part_ref[...] = total(0, 2)
    down_part_ref[...] = total(1, 2)


def relay_kernel(up_ref, down_ref, up_part_ref, down_part_ref, up_out_ref, down_out_ref):
    up_out_ref[0] = (up_ref[0].astype(F32) + up_part_ref[...].astype(F32)).astype(BF16)
    up_out_ref[1] = up_ref[1]
    down_out_ref[0] = down_ref[0]
    down_out_ref[1] = (down_ref[1].astype(F32) + down_part_ref[...].astype(F32)).astype(BF16)


def total_kernel(own_ref, up_ref, down_ref, out_ref):
    units = own_ref.shape[2]
    for i in range(2):
        total = own_ref[i].astype(F32) + up_ref[i].astype(F32) + down_ref[i].astype(F32)
        out_ref[:, 0, i * units : (i + 1) * units] = total


def final_kernel(
    capacity,
    grads_ref,
    col_ref,
    back_ref,
    hidden_ref,
    gate_ref,
    cot_ref,
    router_ref,
    gain_ref,
    block_ref,
    mixer_ref,
):
    del grads_ref
    tokens, width = hidden_ref.shape
    picks = flag(iota((tokens, back_ref.shape[0]), 1) == col_ref[:, :1])
    both = dot(picks, back_ref[...])
    expert_out, dnormed = both[:, :width], both[:, width:]
    gate, cot, hidden = gate_ref[:, :1], cot_ref[...].astype(F32), hidden_ref[...].astype(F32)
    block_ref[...] = (hidden + gate * expert_out).astype(BF16)
    dgate = jnp.sum(cot * expert_out, axis=1, keepdims=True)
    dlogit = dgate * gate * (1.0 - gate)
    chosen = flag(iota((tokens, router_ref.shape[0]), 1) == col_ref[:, :1] // capacity)
    dnormed = dnormed + dlogit * dot(chosen, router_ref[...])
    xhat, inv_std = normal_form(hidden)
    scaled = dnormed * gain_ref[...]
    first = jnp.mean(scaled, axis=-1, keepdims=True)
    second = jnp.mean(scaled * xhat, axis=-1, keepdims=True)
    mixer_ref[...] = cot + inv_std * (scaled - first - xhat * second)


def per_device(
    patches,
    patch_mask,
    mask_token,
    w_qkv,
    w_proj,
    logit_scale,
    rel_bias,
    attn_gain,
    moe_gain,
    router,
    expert_ids,
    w_in,
    w_out,
    cotangent,
):
    height, lateral, width = patches.shape
    tokens = height * lateral
    heads = rel_bias.shape[0]
    expert_total = router.shape[1]
    capacity = 2 * tokens // expert_total
    slot_total = expert_total * capacity
    w_in, w_out = w_in[0], w_out[0]
    units = w_in.shape[1]

    cot = cotangent.reshape(tokens, width)
    router_t = router.T
    dma = pltpu.SemaphoreType.DMA
    masked, right, low, corner = call(
        mask_kernel,
        (
            shape((tokens, width), BF16),
            shape((height * SHIFT, width), BF16),
            shape((SHIFT * lateral, width), BF16),
            shape((SHIFT * SHIFT, width), BF16),
        ),
        (WHOLE,) * 3,
        patches.reshape(tokens, width),
        patch_mask,
        mask_token.reshape(1, width),
    )
    right = passed_along(right, "lon", -1)
    low = passed_along(low, "lat", -1)
    corner = passed_diagonally(corner)

    cot_send, target_row, target_col = call(
        lambda *refs: slot_kernel(expert_total, capacity, *refs),
        (
            far((slot_total, width), BF16),
            shape((1, tokens), I32),
            shape((tokens, 128), I32),
        ),
        (UNREAD, WHOLE, FAR),
        masked,
        expert_ids.reshape(1, tokens),
        kept_far(cot),
        out_specs=(FAR, WHOLE, WHOLE),
        scratch=[
            pltpu.VMEM((tokens, width), BF16),
            pltpu.VMEM((slot_total, width), BF16),
            dma((1,)),
            dma((PARTS,)),
        ],
        flops=2 * slot_total * tokens * width,
    )
    d_slots = exchanged(cot_send.reshape(expert_total, capacity, width)).reshape(slot_total, width)

    last = (lax.axis_index("lat") == lax.axis_size("lat") - 1).astype(I32).reshape(1)
    hidden, normed_send, gate = call(
        lambda *refs: attention_kernel(heads, height, lateral, *refs),
        (
            shape((tokens, width), BF16),
            far((slot_total, width), BF16),
            shape((tokens, 128), F32),
        ),
        (SCALAR,) + (WHOLE,) * 13,
        last,
        masked,
        right,
        low,
        corner,
        w_qkv,
        w_proj,
        logit_scale.reshape(1, heads),
        rel_bias,
        attn_gain.reshape(1, width),
        moe_gain.reshape(1, width),
        router_t,
        target_row,
        target_col,
        out_specs=(WHOLE, FAR, WHOLE),
        scratch=[
            pltpu.VMEM((tokens, width), BF16),
            pltpu.VMEM((slot_total, width), BF16),
            dma((PARTS,)),
        ],
        vmem=28,
        flops=2 * tokens * width * (6 * width + slot_total),
    )
    z_slots = exchanged(normed_send.reshape(expert_total, capacity, width)).reshape(
        slot_total, width
    )
    chunk = units // PARTS
    dact = call(
        early_kernel,
        far((slot_total, units), F32),
        (WHOLE, pl.BlockSpec((width, chunk), lambda i: (0, i))),
        d_slots,
        kept_far(w_out),
        grid=(PARTS,),
        out_specs=pl.BlockSpec((slot_total, chunk), lambda i: (0, i)),
        flops=2 * slot_total * width * units,
    )
    index = jnp.stack([lax.axis_index("lon"), lax.axis_index("lat")]).astype(I32)
    back, activation, dpre = call(
        expert_kernel,
        (
            far((slot_total, 2 * width), BF16),
            far((slot_total, units), BF16),
            far((slot_total, units), BF16),
        ),
        (SCALAR, WHOLE, WHOLE, FAR, FAR, FAR),
        index,
        z_slots,
        router_t,
        kept_far(w_in),
        kept_far(w_out),
        dact,
        out_specs=(FAR, FAR, FAR),
        scratch=[
            pltpu.VMEM((width, units), BF16),
            pltpu.VMEM((width, units), BF16),
            pltpu.VMEM((slot_total, units), F32),
            pltpu.VMEM((slot_total, units), BF16),
            pltpu.VMEM((slot_total, units), BF16),
            pltpu.VMEM((slot_total, 2 * width), BF16),
            dma((2 * PARTS + 1,)),
            dma((3 * PARTS,)),
        ],
        vmem=40,
        flops=6 * slot_total * width * units,
    )
    back = exchanged(back.reshape(expert_total, capacity, 2 * width)).reshape(
        slot_total, 2 * width
    )

    lat_total = lax.axis_size("lat")
    rows = width // lat_total
    half = width // 2
    keep, give = call(
        lambda *refs: grads_kernel(lat_total, *refs),
        (shape((2, half, units), BF16),) * 2,
        (SCALAR, WHOLE, WHOLE, WHOLE) + (pl.BlockSpec((slot_total, chunk), lambda i: (0, i)),) * 2,
        index,
        z_slots,
        d_slots,
        router_t,
        dpre,
        activation,
        grid=(PARTS,),
        out_specs=(pl.BlockSpec((2, half, chunk), lambda i: (0, 0, i)),) * 2,
        scratch=[pltpu.VMEM((width, slot_total), BF16)] * 2,
        vmem=28,
        flops=4 * slot_total * width * units,
    )
    given = lax.ppermute(give, "lat", [(i, i ^ 1) for i in range(lat_total)])
    block, part = shape((2, rows, units), BF16), shape((rows, units), BF16)
    own, up, down, up_part, down_part = call(
        pair_kernel, (block, block, block, part, part), (WHOLE,) * 2, keep, given
    )
    up_part = passed_along(up_part, "lat", 2)
    down_part = passed_along(down_part, "lat", -2)
    up, down = call(relay_kernel, (block, block), (WHOLE,) * 4, up, down, up_part, down_part)
    up = passed_along(up, "lat", 2)
    down = passed_along(down, "lat", -2)
    weight_grads = call(
        total_kernel, far((rows, 1, 2 * units), F32), (WHOLE,) * 3, own, up, down
    )
    span = tokens // PARTS
    tall = pl.BlockSpec((span, width), lambda i: (i, 0))
    thin = pl.BlockSpec((span, 128), lambda i: (i, 0))
    block_out, mixer_grad = call(
        lambda *refs: final_kernel(capacity, *refs),
        (far((tokens, width), BF16), far((tokens, width), F32)),
        (UNREAD, thin, WHOLE, tall, thin, tall, WHOLE, WHOLE),
        weight_grads,
        target_col,
        back,
        hidden,
        gate,
        cot,
        router_t,
        moe_gain.reshape(1, width),
        grid=(PARTS,),
        out_specs=(tall, tall),
        flops=4 * slot_total * tokens * width,
    )
    return (
        block_out.reshape(height, lateral, width),
        mixer_grad.reshape(height, lateral, width),
        weight_grads,
    )


def solution(mesh):
    placed = (
        P("lat", "lon", None),
        P("lat", "lon"),
        P(),
        P(),
        P(),
        P(),
        P(),
        P(),
        P(),
        P(),
        P("lat", "lon", None, None),
        P("lon", None, None),
        P("lon", None, None),
        P("lat", "lon", None),
    )
    return jax.shard_map(
        per_device,
        mesh=mesh,
        in_specs=placed,
        out_specs=(P("lat", "lon", None), P("lat", "lon", None), P("lat", "lon", None)),
        check_vma=False,
    )
```

```python
import math

import jax
import jax.numpy as jnp
from jax import lax
from jax.experimental import pallas as pl
from jax.experimental.pallas import tpu as pltpu
from jax.sharding import PartitionSpec as P

WIN = 8
SHIFT = 4
BF16 = jnp.bfloat16
F32 = jnp.float32
I32 = jnp.int32


MIB = 1024 * 1024
WHOLE = pl.BlockSpec(memory_space=pltpu.VMEM)
SCALAR = pl.BlockSpec(memory_space=pltpu.SMEM)
FAR = pl.BlockSpec(memory_space=pltpu.HBM)
UNREAD = pl.BlockSpec(memory_space=pl.ANY)


def call(body, outs, ins, *operands, scratch=(), grid=(), out_specs=None, vmem=16, flops=0):
    if out_specs is None:
        out_specs = jax.tree.map(lambda _: WHOLE, outs)
    moved = sum(math.prod(x.shape) * x.dtype.itemsize for x in (*operands, *jax.tree.leaves(outs)))
    return pl.pallas_call(
        body,
        grid=grid,
        out_shape=outs,
        in_specs=list(ins),
        out_specs=out_specs,
        scratch_shapes=list(scratch),
        cost_estimate=pl.CostEstimate(
            flops=int(flops), transcendentals=0, bytes_accessed=int(moved)
        ),
        compiler_params=pltpu.CompilerParams(vmem_limit_bytes=vmem * MIB),
    )(*operands)


def shape(dims, dtype):
    return jax.ShapeDtypeStruct(dims, dtype)


def far(dims, dtype):
    return pltpu.HBM(dims, dtype)


def kept_far(array):
    return pltpu.with_memory_space_constraint(array, pltpu.HBM)


def slot_gates(slots, router_t, index):
    logits = dot_nt(slots, router_t)
    mine = iota(logits.shape, 1) == index
    return jax.nn.sigmoid(jnp.sum(jnp.where(mine, logits, 0.0), axis=1, keepdims=True))


def dot(a, b):
    return jnp.dot(a, b, preferred_element_type=F32)


def dot_nt(a, b):
    return lax.dot_general(a, b, (((1,), (1,)), ((), ())), preferred_element_type=F32)


def dot_tn(a, b):
    return lax.dot_general(a, b, (((0,), (0,)), ((), ())), preferred_element_type=F32)


def halves(values):
    high = values.astype(BF16)
    return high, (values - high.astype(F32)).astype(BF16)


def dot_split(values, ones):
    high, low = halves(values)
    return dot(high, ones) + dot(low, ones)


def iota(dims, axis):
    return lax.broadcasted_iota(I32, dims, axis)


def flag(condition):
    return jnp.where(condition, 1.0, 0.0).astype(BF16)


def normal_form(values):
    centred = values - jnp.mean(values, axis=-1, keepdims=True)
    inv_std = lax.rsqrt(jnp.mean(centred * centred, axis=-1, keepdims=True) + 1e-05)
    return centred * inv_std, inv_std


def doubled_gelu_parts(preact):
    scaled = preact * 0.7071067811865476
    doubled_cdf = 1.0 + lax.erf(scaled)
    bell = jnp.exp(-(scaled * scaled))
    return preact * doubled_cdf, doubled_cdf + preact * 0.7978845608028654 * bell


def passed_along(block, axis, distance):
    devices = range(lax.axis_size(axis))
    route = [((i - distance) % len(devices), i) for i in devices]
    return lax.ppermute(block, axis, route)


def passed_diagonally(block):
    rows, columns = lax.axis_size("lat"), lax.axis_size("lon")
    route = [
        ((i + 1) % rows * columns + (j + 1) % columns, i * columns + j)
        for i in range(rows)
        for j in range(columns)
    ]
    return lax.ppermute(block, ("lat", "lon"), route)


def exchanged(slots):
    return lax.all_to_all(slots, "lon", split_axis=0, concat_axis=0, tiled=True)


def send_rows(placed_rows, rows, staged_ref, out_ref, sems):
    copies = []
    for i in range(sems.shape[0]):
        step = out_ref.shape[0] // sems.shape[0]
        part = slice(i * step, (i + 1) * step)
        staged_ref[part] = dot(placed_rows(i * step, step), rows).astype(BF16)
        copies.append(pltpu.make_async_copy(staged_ref.at[part], out_ref.at[part], sems.at[i]))
        copies[-1].start()
    return copies


def slot_kernel(capacity, ids_ref, row_ref, col_ref):
    tokens = ids_ref.shape[1]
    expert_total = 2 * tokens // capacity
    ids = ids_ref[...]
    onehot = iota((expert_total, tokens), 0) == ids
    before = flag(iota((tokens, tokens), 0) < iota((tokens, tokens), 1))
    earlier = dot(flag(onehot), before)
    slot = jnp.sum(jnp.where(onehot, earlier, 0.0), axis=0, keepdims=True).astype(I32)
    target = ids * capacity + slot
    row_ref[...] = target
    diagonal = iota((tokens, tokens), 0) == iota((tokens, tokens), 1)
    column = jnp.sum(jnp.where(diagonal, target, 0).astype(F32), axis=1, keepdims=True)
    col_ref[...] = jnp.broadcast_to(column.astype(I32), col_ref.shape)


def mask_kernel(
    patches_ref,
    mask_ref,
    token_ref,
    masked_ref,
    right_ref,
    low_ref,
    corner_ref,
    patches,
    mask,
    sems,
):
    loads = [
        pltpu.make_async_copy(patches_ref, patches, sems.at[0]),
        pltpu.make_async_copy(mask_ref, mask, sems.at[1]),
    ]
    for load in loads:
        load.start()
    for load in loads:
        load.wait()
    tokens = patches_ref.shape[0]
    height, lateral = mask_ref.shape
    in_row = flag(iota((tokens, height), 0) // lateral == iota((tokens, height), 1))
    spread = dot(in_row, mask[...].astype(F32).astype(BF16))
    own = iota((tokens, lateral), 0) % lateral == iota((tokens, lateral), 1)
    hidden_patch = jnp.sum(jnp.where(own, spread, 0.0), axis=1, keepdims=True)
    masked = jnp.where(
        hidden_patch > 0.5, token_ref[...].astype(F32), patches[...].astype(F32)
    ).astype(BF16)
    masked_ref[...] = masked
    low_ref[...] = masked[: SHIFT * lateral]
    place = iota((height * SHIFT, tokens), 0)
    picks = flag(place // SHIFT * lateral + place % SHIFT == iota((height * SHIFT, tokens), 1))
    right = dot(picks, masked).astype(BF16)
    right_ref[...] = right
    corner_ref[...] = right[: SHIFT * SHIFT]


def attention_kernel(
    heads,
    height,
    lateral,
    flag_ref,
    masked_ref,
    right_ref,
    low_ref,
    corner_ref,
    row_ref,
    qkv_far,
    proj_far,
    scale_far,
    bias_far,
    attn_gain_far,
    moe_gain_far,
    cot_far,
    hidden_ref,
    send_ref,
    qkv_ref,
    proj_ref,
    scale_ref,
    bias_ref,
    attn_gain_ref,
    moe_gain_ref,
    sent_ref,
    blended_ref,
    staged,
    load_sems,
    sems,
):
    loads = [
        pltpu.make_async_copy(source, target, load_sems.at[i])
        for i, (source, target) in enumerate(
            (
                (qkv_far, qkv_ref),
                (scale_far, scale_ref),
                (bias_far, bias_ref),
                (proj_far, proj_ref),
                (attn_gain_far, attn_gain_ref),
                (moe_gain_far, moe_gain_ref),
                (cot_far, sent_ref.at[:, cot_far.shape[1] :]),
            )
        )
    ]
    for load in loads:
        load.start()
    tokens, width = masked_ref.shape
    features = width // heads
    window = WIN * WIN
    across = lateral // WIN
    group = 128 // features

    source = jnp.concatenate([masked_ref[...], right_ref[...], low_ref[...], corner_ref[...]], axis=0)

    place = iota((tokens, 1), 0)
    which, inside = place // window, place % window
    row = which // across * WIN + inside // WIN + SHIFT
    column = which % across * WIN + inside % WIN + SHIFT
    right_base = tokens
    low_base = right_base + height * SHIFT
    corner_base = low_base + SHIFT * lateral
    local = row * lateral + column
    from_right = right_base + row * SHIFT + column - lateral
    from_low = low_base + (row - height) * lateral + column
    from_corner = corner_base + (row - height) * SHIFT + column - lateral
    origin = jnp.where(
        row < height,
        jnp.where(column < lateral, local, from_right),
        jnp.where(column < lateral, from_low, from_corner),
    )
    moves = flag(iota((tokens, source.shape[0]), 1) == origin)
    displaced_f = dot(moves, source)
    displaced = displaced_f.astype(BF16)

    loads[0].wait()
    projected = dot(displaced, qkv_ref[...]).astype(BF16)
    head_of = flag(iota((width, heads), 0) // features == iota((width, heads), 1))
    of_head = flag(iota((heads, width), 1) // features == iota((heads, width), 0))
    loads[1].wait()
    queries = projected[:, :width].astype(F32)
    keys = projected[:, width : 2 * width].astype(F32)
    query_norm = lax.rsqrt(dot_split(queries * queries, head_of) + 1e-06) * scale_ref[...]
    key_norm = lax.rsqrt(dot_split(keys * keys, head_of) + 1e-06)
    queries = (queries * dot_split(query_norm, of_head)).astype(BF16)
    keys = (keys * dot_split(key_norm, of_head)).astype(BF16)

    block = group * window
    loads[2].wait()
    biases = [
        jnp.concatenate([bias_ref[g * group + i] for i in range(group)], axis=1)
        for g in range(width // 128)
    ]
    member = flag(
        iota((block, 128), 0) // window == iota((block, 128), 1) // features
    )
    split = (iota((window, block), 0) >= window // 2) == (
        iota((window, block), 1) % window >= window // 2
    )
    allowed = jnp.where(split, 1.0, jnp.where(flag_ref[0] == 1, 0.0, 1.0))
    for w in range(tokens // window):
        rows = slice(w * window, (w + 1) * window)
        for g in range(width // 128):
            lanes = slice(g * 128, (g + 1) * 128)
            q = queries[rows, lanes]
            k = keys[rows, lanes]
            v = projected[rows, 2 * width + g * 128 : 2 * width + (g + 1) * 128]
            wide_k = jnp.concatenate([k] * group, axis=0) * member
            wide_v = jnp.concatenate([v] * group, axis=0) * member
            scores = dot_nt(q, wide_k) + biases[g]
            weights = jnp.exp(scores)
            if w >= across * (height // WIN - 1):
                weights = weights * allowed
            both = dot(weights.astype(BF16), jnp.concatenate([wide_v, member], axis=1))
            blended_ref[rows, lanes] = (both[:, :128] / both[:, 128:]).astype(BF16)

    for load in loads[3:]:
        load.wait()
    projection = dot(blended_ref[...], proj_ref[...])
    branch, _ = normal_form(projection)
    hidden = displaced_f + branch * attn_gain_ref[...]
    hidden = hidden.reshape(height // WIN, across, WIN, WIN, width).transpose(0, 2, 1, 3, 4)
    hidden = hidden.reshape(tokens, width).astype(BF16)
    hidden_ref[...] = hidden
    normed, _ = normal_form(hidden.astype(F32))
    sent_ref[:, :width] = (normed * moe_gain_ref[...]).astype(BF16)
    copies = send_rows(
        lambda start, step: flag(iota((step, tokens), 0) + start == row_ref[...]),
        sent_ref[...],
        staged,
        send_ref,
        sems,
    )
    for copy in copies:
        copy.wait()


PARTS = 4


def expert_kernel(
    index_ref,
    slots_ref,
    router_ref,
    w_in_ref,
    w_out_ref,
    back_ref,
    act_ref,
    dpre_ref,
    w_in,
    w_out,
    act,
    dpre,
    back,
    load_sems,
    store_sems,
):
    rows, width = slots_ref.shape[0], slots_ref.shape[1] // 2
    units = w_in.shape[1]
    tile, chunk, piece = rows // PARTS, units // PARTS, width // 2

    def load(source, target, i):
        copy = pltpu.make_async_copy(source, target, load_sems.at[i])
        copy.start()
        return copy

    def tiled(i, step):
        return slice(i * step, (i + 1) * step)

    loads = []
    for i in range(PARTS):
        part = tiled(i, chunk)
        loads.append(load(w_in_ref.at[:, part], w_in.at[:, part], 2 * i))
        loads.append(load(w_out_ref.at[:, part], w_out.at[:, part], 2 * i + 1))
    half_gate = 0.5 * slot_gates(slots_ref[:, :width], router_ref[...], index_ref[0])
    stores = []

    def store(source, target):
        copy = pltpu.make_async_copy(source, target, store_sems.at[len(stores)])
        copy.start()
        stores.append(copy)

    for r in range(PARTS + 1):
        here, last = tiled(r, tile), tiled(r - 1, tile)
        for c in range(PARTS):
            part = tiled(c, chunk)
            if r < PARTS:
                if r == 0:
                    loads[2 * c].wait()
                    loads[2 * c + 1].wait()
                activation, slopes = doubled_gelu_parts(
                    dot(slots_ref[here, :width], w_in[:, part])
                )
                act[here, part] = activation.astype(BF16)
                dact = dot(slots_ref[here, width:], w_out[:, part])
                dpre[here, part] = (dact * slopes).astype(BF16)
            if r > 0:
                half = tiled(c % 2, piece)
                if c < 2:
                    result = 0.5 * dot_nt(act[last], w_out[half])
                else:
                    result = half_gate[last] * dot_nt(dpre[last], w_in[half])
                back[last, tiled(c, piece)] = result.astype(BF16)
        if r < PARTS:
            store(act.at[here], act_ref.at[here])
            store(dpre.at[here], dpre_ref.at[here])
        if r > 0:
            store(back.at[last], back_ref.at[last])
    for copy in stores:
        copy.wait()


def grads_kernel(
    lat_total, index_ref, slots_ref, router_ref, dpre_ref, act_ref, keep_ref, give_ref, zt, dt
):
    width = slots_ref.shape[1] // 2
    rows = width // lat_total

    @pl.when(pl.program_id(0) == 0)
    def _():
        place = iota((width, 1), 0)
        half, step, inside = place // (width // 2), place % (width // 2) // rows, place % rows
        column, core = index_ref[1] // 2, index_ref[1] % 2
        block = (step + column) % (lat_total // 2) * 2 + (half + core) % 2
        moves = flag(iota((width, width), 1) == block * rows + inside)
        half_gate = 0.5 * slot_gates(slots_ref[:, :width], router_ref[...], index_ref[0])
        for i, turned in enumerate((zt, dt)):
            part = slots_ref[:, i * width : (i + 1) * width]
            scaled = (part.astype(F32) * half_gate).astype(BF16)
            turned[...] = dot_nt(moves, scaled).astype(BF16)

    for i, (left, right) in enumerate(((zt, dpre_ref), (dt, act_ref))):
        total = dot(left[...], right[...]).astype(BF16)
        keep_ref[i] = total[: width // 2]
        give_ref[i] = total[width // 2 :]


def pair_kernel(keep_ref, given_ref, own_ref, up_ref, down_ref, up_part_ref, down_part_ref):
    rows = own_ref.shape[1]

    def total(i, step):
        part = slice(step * rows, (step + 1) * rows)
        return (keep_ref[i, part].astype(F32) + given_ref[i, part].astype(F32)).astype(BF16)

    for i in range(2):
        own_ref[i] = total(i, 0)
        up_ref[i] = total(i, 1)
        down_ref[i] = total(i, 3)
    up_part_ref[...] = total(0, 2)
    down_part_ref[...] = total(1, 2)


def relay_kernel(up_ref, down_ref, up_part_ref, down_part_ref, up_out_ref, down_out_ref):
    up_out_ref[0] = (up_ref[0].astype(F32) + up_part_ref[...].astype(F32)).astype(BF16)
    up_out_ref[1] = up_ref[1]
    down_out_ref[0] = down_ref[0]
    down_out_ref[1] = (down_ref[1].astype(F32) + down_part_ref[...].astype(F32)).astype(BF16)


def total_kernel(own_ref, up_ref, down_ref, out_ref):
    units = own_ref.shape[2]
    for i in range(2):
        total = own_ref[i].astype(F32) + up_ref[i].astype(F32) + down_ref[i].astype(F32)
        out_ref[:, 0, i * units : (i + 1) * units] = total


def ready_kernel(
    capacity, col_ref, hidden_ref, router_ref, gain_ref, picks_ref, xhat_ref, gate_ref, inv_ref
):
    tokens = hidden_ref.shape[0]
    picks_ref[...] = flag(iota(picks_ref.shape, 1) == col_ref[:, :1])
    xhat, inv_std = normal_form(hidden_ref[...].astype(F32))
    xhat_ref[...] = xhat
    inv_ref[...] = jnp.broadcast_to(inv_std, inv_ref.shape)
    chosen = iota((tokens, router_ref.shape[0]), 1) == col_ref[:, :1] // capacity
    logits = dot_nt((xhat * gain_ref[...]).astype(BF16), router_ref[...])
    gate = jax.nn.sigmoid(jnp.sum(jnp.where(chosen, logits, 0.0), axis=1, keepdims=True))
    gate_ref[...] = jnp.broadcast_to(gate, gate_ref.shape)


def final_kernel(
    capacity,
    grads_ref,
    picks_ref,
    xhat_ref,
    gate_ref,
    inv_ref,
    col_ref,
    back_ref,
    hidden_ref,
    cot_ref,
    router_ref,
    gain_ref,
    block_ref,
    mixer_ref,
    block,
    mixer,
    sems,
):
    del grads_ref
    tokens, width = hidden_ref.shape
    span = tokens // PARTS
    copies = []
    for i in range(PARTS):
        here = slice(i * span, (i + 1) * span)
        both = dot(picks_ref[here], back_ref[...])
        expert_out, dnormed = both[:, :width], both[:, width:]
        gate, cot = gate_ref[here, :1], cot_ref[here].astype(F32)
        block[here] = (hidden_ref[here].astype(F32) + gate * expert_out).astype(BF16)
        dlogit = jnp.sum(cot * expert_out, axis=1, keepdims=True) * gate * (1.0 - gate)
        chosen = flag(iota((span, router_ref.shape[0]), 1) == col_ref[here, :1] // capacity)
        dnormed = dnormed + dlogit * dot(chosen, router_ref[...])
        scaled, xhat = dnormed * gain_ref[...], xhat_ref[here]
        first = jnp.mean(scaled, axis=-1, keepdims=True)
        second = jnp.mean(scaled * xhat, axis=-1, keepdims=True)
        mixer[here] = cot + inv_ref[here, :1] * (scaled - first - xhat * second)
        for j, (source, target) in enumerate(((block, block_ref), (mixer, mixer_ref))):
            copies.append(pltpu.make_async_copy(source.at[here], target.at[here], sems.at[i, j]))
            copies[-1].start()
    for copy in copies:
        copy.wait()


def per_device(
    patches,
    patch_mask,
    mask_token,
    w_qkv,
    w_proj,
    logit_scale,
    rel_bias,
    attn_gain,
    moe_gain,
    router,
    expert_ids,
    w_in,
    w_out,
    cotangent,
):
    height, lateral, width = patches.shape
    tokens = height * lateral
    heads = rel_bias.shape[0]
    expert_total = router.shape[1]
    capacity = 2 * tokens // expert_total
    slot_total = expert_total * capacity
    w_in, w_out = w_in[0], w_out[0]
    units = w_in.shape[1]

    dma = pltpu.SemaphoreType.DMA
    cot = cotangent.reshape(tokens, width)
    router_t = router.T
    masked, right, low, corner = call(
        mask_kernel,
        (
            shape((tokens, width), BF16),
            far((height * SHIFT, width), BF16),
            far((SHIFT * lateral, width), BF16),
            far((SHIFT * SHIFT, width), BF16),
        ),
        (FAR, FAR, WHOLE),
        kept_far(patches.reshape(tokens, width)),
        kept_far(patch_mask),
        mask_token.reshape(1, width),
        scratch=[
            pltpu.VMEM((tokens, width), BF16),
            pltpu.VMEM((height, lateral), I32),
            dma((2,)),
        ],
    )
    right = passed_along(right, "lon", -1)
    low = passed_along(low, "lat", -1)
    corner = passed_diagonally(corner)

    target_row, target_col = call(
        lambda *refs: slot_kernel(capacity, *refs),
        (shape((1, tokens), I32), shape((tokens, 128), I32)),
        (WHOLE,),
        expert_ids.reshape(1, tokens),
    )
    last = (lax.axis_index("lat") == lax.axis_size("lat") - 1).astype(I32).reshape(1)
    hidden, send = call(
        lambda *refs: attention_kernel(heads, height, lateral, *refs),
        (
            far((tokens, width), BF16),
            far((slot_total, 2 * width), BF16),
        ),
        (SCALAR,) + (WHOLE,) * 5 + (FAR,) * 7,
        last,
        masked,
        right,
        low,
        corner,
        target_row,
        kept_far(w_qkv),
        kept_far(w_proj),
        kept_far(logit_scale.reshape(1, heads)),
        kept_far(rel_bias),
        kept_far(attn_gain.reshape(1, width)),
        kept_far(moe_gain.reshape(1, width)),
        kept_far(cot),
        out_specs=(WHOLE, FAR),
        scratch=[
            pltpu.VMEM(w_qkv.shape, BF16),
            pltpu.VMEM(w_proj.shape, BF16),
            pltpu.VMEM((1, heads), F32),
            pltpu.VMEM(rel_bias.shape, F32),
            pltpu.VMEM((1, width), F32),
            pltpu.VMEM((1, width), F32),
            pltpu.VMEM((tokens, 2 * width), BF16),
            pltpu.VMEM((tokens, width), BF16),
            pltpu.VMEM((slot_total, 2 * width), BF16),
            dma((7,)),
            dma((PARTS,)),
        ],
        vmem=32,
        flops=2 * tokens * width * (6 * width + 2 * slot_total),
    )
    slots = exchanged(send.reshape(expert_total, capacity, 2 * width)).reshape(
        slot_total, 2 * width
    )
    chunk = units // PARTS
    index = jnp.stack([lax.axis_index("lon"), lax.axis_index("lat")]).astype(I32)
    back, activation, dpre = call(
        expert_kernel,
        (
            far((slot_total, 2 * width), BF16),
            far((slot_total, units), BF16),
            far((slot_total, units), BF16),
        ),
        (SCALAR, WHOLE, WHOLE, FAR, FAR),
        index,
        slots,
        router_t,
        kept_far(w_in),
        kept_far(w_out),
        out_specs=(FAR, FAR, FAR),
        scratch=[
            pltpu.VMEM((width, units), BF16),
            pltpu.VMEM((width, units), BF16),
            pltpu.VMEM((slot_total, units), BF16),
            pltpu.VMEM((slot_total, units), BF16),
            pltpu.VMEM((slot_total, 2 * width), BF16),
            dma((2 * PARTS,)),
            dma((3 * PARTS,)),
        ],
        vmem=40,
        flops=8 * slot_total * width * units,
    )
    back = exchanged(back.reshape(expert_total, capacity, 2 * width)).reshape(
        slot_total, 2 * width
    )

    lat_total = lax.axis_size("lat")
    rows = width // lat_total
    half = width // 2
    keep, give = call(
        lambda *refs: grads_kernel(lat_total, *refs),
        (shape((2, half, units), BF16),) * 2,
        (SCALAR, WHOLE, WHOLE) + (pl.BlockSpec((slot_total, chunk), lambda i: (0, i)),) * 2,
        index,
        slots,
        router_t,
        kept_far(dpre),
        kept_far(activation),
        grid=(PARTS,),
        out_specs=(pl.BlockSpec((2, half, chunk), lambda i: (0, 0, i)),) * 2,
        scratch=[pltpu.VMEM((width, slot_total), BF16)] * 2,
        vmem=28,
        flops=4 * slot_total * width * units,
    )
    given = lax.ppermute(give, "lat", [(i, i ^ 1) for i in range(lat_total)])
    block, part = shape((2, rows, units), BF16), shape((rows, units), BF16)
    own, up, down, up_part, down_part = call(
        pair_kernel, (block, block, block, part, part), (WHOLE,) * 2, keep, given
    )
    up_part = passed_along(up_part, "lat", 2)
    down_part = passed_along(down_part, "lat", -2)
    up, down = call(relay_kernel, (block, block), (WHOLE,) * 4, up, down, up_part, down_part)
    up = passed_along(up, "lat", 2)
    down = passed_along(down, "lat", -2)
    weight_grads = call(
        total_kernel, far((rows, 1, 2 * units), F32), (WHOLE,) * 3, own, up, down
    )
    moe_row = moe_gain.reshape(1, width)
    thin = shape((tokens, 128), F32)
    picks, xhat, gate, inv_std = call(
        lambda *refs: ready_kernel(capacity, *refs),
        (shape((tokens, slot_total), BF16), shape((tokens, width), F32), thin, thin),
        (WHOLE,) * 4,
        target_col,
        hidden,
        router_t,
        moe_row,
        flops=2 * tokens * slot_total * width,
    )
    block_out, mixer_grad = call(
        lambda *refs: final_kernel(capacity, *refs),
        (far((tokens, width), BF16), far((tokens, width), F32)),
        (UNREAD,) + (WHOLE,) * 10,
        kept_far(weight_grads),
        picks,
        xhat,
        gate,
        inv_std,
        target_col,
        back,
        hidden,
        cot,
        router_t,
        moe_row,
        out_specs=(FAR, FAR),
        scratch=[
            pltpu.VMEM((tokens, width), BF16),
            pltpu.VMEM((tokens, width), F32),
            dma((PARTS, 2)),
        ],
        flops=4 * slot_total * tokens * width,
    )
    return (
        block_out.reshape(height, lateral, width),
        mixer_grad.reshape(height, lateral, width),
        weight_grads,
    )


def solution(mesh):
    placed = (
        P("lat", "lon", None),
        P("lat", "lon"),
        P(),
        P(),
        P(),
        P(),
        P(),
        P(),
        P(),
        P(),
        P("lat", "lon", None, None),
        P("lon", None, None),
        P("lon", None, None),
        P("lat", "lon", None),
    )
    return jax.shard_map(
        per_device,
        mesh=mesh,
        in_specs=placed,
        out_specs=(P("lat", "lon", None), P("lat", "lon", None), P("lat", "lon", None)),
        check_vma=False,
    )
```

```python
import math

import jax
import jax.numpy as jnp
from jax import lax
from jax.experimental import pallas as pl
from jax.experimental.pallas import tpu as pltpu
from jax.sharding import PartitionSpec as P

WIN = 8
SHIFT = 4
BF16 = jnp.bfloat16
F32 = jnp.float32
I32 = jnp.int32


MIB = 1024 * 1024
WHOLE = pl.BlockSpec(memory_space=pltpu.VMEM)
SCALAR = pl.BlockSpec(memory_space=pltpu.SMEM)
FAR = pl.BlockSpec(memory_space=pltpu.HBM)
UNREAD = pl.BlockSpec(memory_space=pl.ANY)


def call(
    body, outs, ins, *operands, scratch=(), grid=(), out_specs=None, vmem=16, flops=0, aliases=None
):
    if out_specs is None:
        out_specs = jax.tree.map(lambda _: WHOLE, outs)
    moved = sum(math.prod(x.shape) * x.dtype.itemsize for x in (*operands, *jax.tree.leaves(outs)))
    return pl.pallas_call(
        body,
        grid=grid,
        out_shape=outs,
        in_specs=list(ins),
        out_specs=out_specs,
        scratch_shapes=list(scratch),
        input_output_aliases=aliases or {},
        cost_estimate=pl.CostEstimate(
            flops=int(flops), transcendentals=0, bytes_accessed=int(moved)
        ),
        compiler_params=pltpu.CompilerParams(vmem_limit_bytes=vmem * MIB),
    )(*operands)


def shape(dims, dtype):
    return jax.ShapeDtypeStruct(dims, dtype)


def far(dims, dtype):
    return pltpu.HBM(dims, dtype)


def kept_far(array):
    return pltpu.with_memory_space_constraint(array, pltpu.HBM)


def slot_gates(slots, router_t, index):
    logits = dot_nt(slots, router_t)
    mine = iota(logits.shape, 1) == index
    return jax.nn.sigmoid(jnp.sum(jnp.where(mine, logits, 0.0), axis=1, keepdims=True))


def dot(a, b):
    return jnp.dot(a, b, preferred_element_type=F32)


def dot_nt(a, b):
    return lax.dot_general(a, b, (((1,), (1,)), ((), ())), preferred_element_type=F32)


def dot_tn(a, b):
    return lax.dot_general(a, b, (((0,), (0,)), ((), ())), preferred_element_type=F32)


def halves(values):
    high = values.astype(BF16)
    return high, (values - high.astype(F32)).astype(BF16)


def dot_split(values, ones):
    high, low = halves(values)
    return dot(high, ones) + dot(low, ones)


def iota(dims, axis):
    return lax.broadcasted_iota(I32, dims, axis)


def flag(condition):
    return jnp.where(condition, 1.0, 0.0).astype(BF16)


def normal_form(values):
    centred = values - jnp.mean(values, axis=-1, keepdims=True)
    inv_std = lax.rsqrt(jnp.mean(centred * centred, axis=-1, keepdims=True) + 1e-05)
    return centred * inv_std, inv_std


def doubled_gelu_parts(preact):
    scaled = preact * 0.7071067811865476
    doubled_cdf = 1.0 + lax.erf(scaled)
    bell = jnp.exp(-(scaled * scaled))
    return preact * doubled_cdf, doubled_cdf + preact * 0.7978845608028654 * bell


def passed_along(block, axis, distance):
    devices = range(lax.axis_size(axis))
    route = [((i - distance) % len(devices), i) for i in devices]
    return lax.ppermute(block, axis, route)


def passed_diagonally(block):
    rows, columns = lax.axis_size("lat"), lax.axis_size("lon")
    route = [
        ((i + 1) % rows * columns + (j + 1) % columns, i * columns + j)
        for i in range(rows)
        for j in range(columns)
    ]
    return lax.ppermute(block, ("lat", "lon"), route)


def exchanged(slots):
    return lax.all_to_all(slots, "lon", split_axis=0, concat_axis=0, tiled=True)


def send_rows(placed_ref, rows, staged_ref, out_ref, sems):
    copies = []
    step = out_ref.shape[0] // sems.shape[0]
    for i in range(sems.shape[0]):
        part = slice(i * step, (i + 1) * step)
        staged_ref[part] = dot(placed_ref[part], rows).astype(BF16)
        copies.append(pltpu.make_async_copy(staged_ref.at[part], out_ref.at[part], sems.at[i]))
        copies[-1].start()
    return copies


def origins(tokens, height, lateral):
    across = lateral // WIN
    place = iota((tokens, 1), 0)
    which, inside = place // (WIN * WIN), place % (WIN * WIN)
    row = which // across * WIN + inside // WIN + SHIFT
    column = which % across * WIN + inside % WIN + SHIFT
    right_base = tokens
    low_base = right_base + height * SHIFT
    corner_base = low_base + SHIFT * lateral
    local = row * lateral + column
    from_right = right_base + row * SHIFT + column - lateral
    from_low = low_base + (row - height) * lateral + column
    from_corner = corner_base + (row - height) * SHIFT + column - lateral
    return jnp.where(
        row < height,
        jnp.where(column < lateral, local, from_right),
        jnp.where(column < lateral, from_low, from_corner),
    )


def plan_kernel(
    expert_total,
    height,
    lateral,
    ids_far,
    cot_far,
    col_ref,
    placed_ref,
    moves_ref,
    send_ref,
    ids_ref,
    cot_ref,
    staged,
    load_sems,
    sems,
):
    load_ids = pltpu.make_async_copy(ids_far, ids_ref, load_sems.at[0])
    load_cot = pltpu.make_async_copy(cot_far, cot_ref, load_sems.at[1])
    load_ids.start()
    load_cot.start()
    tokens, width = cot_ref.shape
    slot_total = placed_ref.shape[0]
    moves_ref[...] = flag(iota(moves_ref.shape, 1) == origins(tokens, height, lateral))
    before = flag(iota((tokens, tokens), 0) < iota((tokens, tokens), 1))
    load_ids.wait()
    ids = ids_ref[...]
    onehot = iota((expert_total, tokens), 0) == ids
    earlier = dot(flag(onehot), before)
    slot = jnp.sum(jnp.where(onehot, earlier, 0.0), axis=0, keepdims=True).astype(I32)
    target = ids * (slot_total // expert_total) + slot
    placed_ref[...] = flag(iota(placed_ref.shape, 0) == target)
    load_cot.wait()
    copies = send_rows(placed_ref, cot_ref[...], staged, send_ref.at[:, width:], sems)
    diagonal = iota((tokens, tokens), 0) == iota((tokens, tokens), 1)
    column = jnp.sum(jnp.where(diagonal, target, 0).astype(F32), axis=1, keepdims=True)
    col_ref[...] = jnp.broadcast_to(column.astype(I32), col_ref.shape)
    for copy in copies:
        copy.wait()


def mask_kernel(
    patches_ref,
    mask_ref,
    token_ref,
    masked_ref,
    right_ref,
    low_ref,
    corner_ref,
    patches,
    mask,
    sems,
):
    loads = [
        pltpu.make_async_copy(patches_ref, patches, sems.at[0]),
        pltpu.make_async_copy(mask_ref, mask, sems.at[1]),
    ]
    for load in loads:
        load.start()
    for load in loads:
        load.wait()
    tokens = patches_ref.shape[0]
    height, lateral = mask_ref.shape
    in_row = flag(iota((tokens, height), 0) // lateral == iota((tokens, height), 1))
    spread = dot(in_row, mask[...].astype(F32).astype(BF16))
    own = iota((tokens, lateral), 0) % lateral == iota((tokens, lateral), 1)
    hidden_patch = jnp.sum(jnp.where(own, spread, 0.0), axis=1, keepdims=True)
    masked = jnp.where(
        hidden_patch > 0.5, token_ref[...].astype(F32)[None, :], patches[...].astype(F32)
    ).astype(BF16)
    masked_ref[...] = masked
    low_ref[...] = masked[: SHIFT * lateral]
    place = iota((height * SHIFT, tokens), 0)
    picks = flag(place // SHIFT * lateral + place % SHIFT == iota((height * SHIFT, tokens), 1))
    right = dot(picks, masked).astype(BF16)
    right_ref[...] = right
    corner_ref[...] = right[: SHIFT * SHIFT]


def attention_kernel(
    heads,
    height,
    lateral,
    flag_ref,
    masked_ref,
    right_ref,
    low_ref,
    corner_ref,
    placed_ref,
    moves_ref,
    sent_far,
    qkv_far,
    proj_far,
    scale_far,
    bias_far,
    attn_gain_far,
    moe_gain_far,
    hidden_ref,
    send_ref,
    qkv_ref,
    proj_ref,
    scale_ref,
    bias_ref,
    attn_gain_ref,
    moe_gain_ref,
    blended_ref,
    staged,
    load_sems,
    sems,
):
    del sent_far
    loads = [
        pltpu.make_async_copy(source, target, load_sems.at[i])
        for i, (source, target) in enumerate(
            (
                (qkv_far, qkv_ref),
                (scale_far, scale_ref),
                (bias_far, bias_ref),
                (proj_far, proj_ref),
                (attn_gain_far, attn_gain_ref),
                (moe_gain_far, moe_gain_ref),
            )
        )
    ]
    for load in loads:
        load.start()
    tokens, width = masked_ref.shape
    features = width // heads
    window = WIN * WIN
    across = lateral // WIN
    group = 128 // features

    source = jnp.concatenate([masked_ref[...], right_ref[...], low_ref[...], corner_ref[...]], axis=0)

    displaced_f = dot(moves_ref[...], source)
    displaced = displaced_f.astype(BF16)

    loads[0].wait()
    projected = dot(displaced, qkv_ref[...]).astype(BF16)
    head_of = flag(iota((width, heads), 0) // features == iota((width, heads), 1))
    of_head = flag(iota((heads, width), 1) // features == iota((heads, width), 0))
    loads[1].wait()
    queries = projected[:, :width].astype(F32)
    keys = projected[:, width : 2 * width].astype(F32)
    query_norm = lax.rsqrt(dot((queries * queries).astype(BF16), head_of) + 1e-06) * scale_ref[...]
    key_norm = lax.rsqrt(dot((keys * keys).astype(BF16), head_of) + 1e-06)
    queries = (queries * dot_split(query_norm, of_head)).astype(BF16)
    keys = (keys * dot_split(key_norm, of_head)).astype(BF16)

    block = group * window
    loads[2].wait()
    biases = [
        jnp.concatenate([bias_ref[g * group + i] for i in range(group)], axis=1)
        for g in range(width // 128)
    ]
    member = flag(
        iota((block, 128), 0) // window == iota((block, 128), 1) // features
    )
    split = (iota((window, block), 0) >= window // 2) == (
        iota((window, block), 1) % window >= window // 2
    )
    allowed = jnp.where(split, 1.0, jnp.where(flag_ref[0] == 1, 0.0, 1.0))
    for w in range(tokens // window):
        rows = slice(w * window, (w + 1) * window)
        for g in range(width // 128):
            lanes = slice(g * 128, (g + 1) * 128)
            q = queries[rows, lanes]
            k = keys[rows, lanes]
            v = projected[rows, 2 * width + g * 128 : 2 * width + (g + 1) * 128]
            wide_k = jnp.concatenate([k] * group, axis=0) * member
            wide_v = jnp.concatenate([v] * group, axis=0) * member
            scores = dot_nt(q, wide_k) + biases[g]
            weights = jnp.exp(scores)
            if w >= across * (height // WIN - 1):
                weights = weights * allowed
            both = dot(weights.astype(BF16), jnp.concatenate([wide_v, member], axis=1))
            blended_ref[rows, lanes] = (both[:, :128] / both[:, 128:]).astype(BF16)

    for load in loads[3:]:
        load.wait()
    projection = dot(blended_ref[...], proj_ref[...])
    branch, _ = normal_form(projection)
    hidden = displaced_f + branch * attn_gain_ref[...]
    hidden = hidden.reshape(height // WIN, across, WIN, WIN, width).transpose(0, 2, 1, 3, 4)
    hidden = hidden.reshape(tokens, width).astype(BF16)
    hidden_ref[...] = hidden
    normed, _ = normal_form(hidden.astype(F32))
    normed = (normed * moe_gain_ref[...]).astype(BF16)
    copies = send_rows(placed_ref, normed, staged, send_ref.at[:, :width], sems)
    for copy in copies:
        copy.wait()


PARTS = 4


def expert_kernel(
    index_ref,
    slots_ref,
    router_ref,
    w_in_ref,
    w_out_ref,
    back_ref,
    act_ref,
    dpre_ref,
    w_in,
    w_out,
    act,
    dpre,
    back,
    load_sems,
    store_sems,
):
    rows, width = slots_ref.shape[0], slots_ref.shape[1] // 2
    units = w_in.shape[1]
    tile, chunk, piece = rows // PARTS, units // PARTS, width // 2

    def load(source, target, i):
        copy = pltpu.make_async_copy(source, target, load_sems.at[i])
        copy.start()
        return copy

    def tiled(i, step):
        return slice(i * step, (i + 1) * step)

    loads = []
    for i in range(PARTS):
        part = tiled(i, chunk)
        loads.append(load(w_in_ref.at[:, part], w_in.at[:, part], 2 * i))
        loads.append(load(w_out_ref.at[:, part], w_out.at[:, part], 2 * i + 1))
    half_gate = 0.5 * slot_gates(slots_ref[:, :width], router_ref[...], index_ref[0])
    stores = []

    def store(source, target):
        copy = pltpu.make_async_copy(source, target, store_sems.at[len(stores)])
        copy.start()
        stores.append(copy)

    for r in range(PARTS + 1):
        here, last = tiled(r, tile), tiled(r - 1, tile)
        for c in range(PARTS):
            part = tiled(c, chunk)
            if r < PARTS:
                if r == 0:
                    loads[2 * c].wait()
                    loads[2 * c + 1].wait()
                activation, slopes = doubled_gelu_parts(
                    dot(slots_ref[here, :width], w_in[:, part])
                )
                act[here, part] = activation.astype(BF16)
                dact = dot(slots_ref[here, width:], w_out[:, part])
                dpre[here, part] = (dact * slopes).astype(BF16)
            if r > 0:
                half = tiled(c % 2, piece)
                if c < 2:
                    result = 0.5 * dot_nt(act[last], w_out[half])
                else:
                    result = half_gate[last] * dot_nt(dpre[last], w_in[half])
                back[last, tiled(c, piece)] = result.astype(BF16)
        if r < PARTS:
            store(act.at[here], act_ref.at[here])
            store(dpre.at[here], dpre_ref.at[here])
        if r > 0:
            store(back.at[last], back_ref.at[last])
    for copy in stores:
        copy.wait()


def grads_kernel(
    lat_total, index_ref, slots_ref, router_ref, dpre_ref, act_ref, keep_ref, give_ref, zt, dt
):
    width = slots_ref.shape[1] // 2
    rows = width // lat_total

    @pl.when(pl.program_id(0) == 0)
    def _():
        place = iota((width, 1), 0)
        half, step, inside = place // (width // 2), place % (width // 2) // rows, place % rows
        column, core = index_ref[1] // 2, index_ref[1] % 2
        block = (step + column) % (lat_total // 2) * 2 + (half + core) % 2
        moves = flag(iota((width, width), 1) == block * rows + inside)
        half_gate = 0.5 * slot_gates(slots_ref[:, :width], router_ref[...], index_ref[0])
        for i, turned in enumerate((zt, dt)):
            part = slots_ref[:, i * width : (i + 1) * width]
            scaled = (part.astype(F32) * half_gate).astype(BF16)
            turned[...] = dot_nt(moves, scaled).astype(BF16)

    for i, (left, right) in enumerate(((zt, dpre_ref), (dt, act_ref))):
        total = dot(left[...], right[...]).astype(BF16)
        keep_ref[i] = total[: width // 2]
        give_ref[i] = total[width // 2 :]


def pair_kernel(keep_ref, given_ref, own_ref, up_ref, down_ref, up_part_ref, down_part_ref):
    rows = own_ref.shape[1]

    def total(i, step):
        part = slice(step * rows, (step + 1) * rows)
        return (keep_ref[i, part].astype(F32) + given_ref[i, part].astype(F32)).astype(BF16)

    for i in range(2):
        own_ref[i] = total(i, 0)
        up_ref[i] = total(i, 1)
        down_ref[i] = total(i, 3)
    up_part_ref[...] = total(0, 2)
    down_part_ref[...] = total(1, 2)


def relay_kernel(up_ref, down_ref, up_part_ref, down_part_ref, up_out_ref, down_out_ref):
    up_out_ref[0] = (up_ref[0].astype(F32) + up_part_ref[...].astype(F32)).astype(BF16)
    up_out_ref[1] = up_ref[1]
    down_out_ref[0] = down_ref[0]
    down_out_ref[1] = (down_ref[1].astype(F32) + down_part_ref[...].astype(F32)).astype(BF16)


def total_kernel(own_ref, up_ref, down_ref, out_ref):
    units = own_ref.shape[2]
    for i in range(2):
        total = own_ref[i].astype(F32) + up_ref[i].astype(F32) + down_ref[i].astype(F32)
        out_ref[:, 0, i * units : (i + 1) * units] = total


def ready_kernel(capacity, col_ref, hidden_ref, router_ref, gain_ref, facts_ref):
    tokens = hidden_ref.shape[0]
    hidden = hidden_ref[...].astype(F32)
    average = jnp.mean(hidden, axis=-1, keepdims=True)
    xhat, inv_std = normal_form(hidden)
    target = col_ref[:, :1]
    chosen = iota((tokens, router_ref.shape[0]), 1) == target // capacity
    logits = dot_nt((xhat * gain_ref[...]).astype(BF16), router_ref[...])
    gate = jax.nn.sigmoid(jnp.sum(jnp.where(chosen, logits, 0.0), axis=1, keepdims=True))
    lane = iota(facts_ref.shape, 1)
    facts = jnp.where(lane == 0, target.astype(F32), gate)
    facts_ref[...] = jnp.where(lane == 2, average, jnp.where(lane == 3, inv_std, facts))


def final_kernel(
    capacity,
    grads_ref,
    facts_far,
    hidden_far,
    cot_far,
    router_far,
    gain_far,
    back_ref,
    block_ref,
    mixer_ref,
    facts_ref,
    hidden_ref,
    cot_ref,
    router_ref,
    gain_ref,
    block,
    mixer,
    load_sems,
    sems,
):
    del grads_ref
    loads = [
        pltpu.make_async_copy(source, target, load_sems.at[i])
        for i, (source, target) in enumerate(
            (
                (facts_far, facts_ref),
                (hidden_far, hidden_ref),
                (cot_far, cot_ref),
                (router_far, router_ref),
                (gain_far, gain_ref),
            )
        )
    ]
    for load in loads:
        load.start()
    tokens, width = hidden_ref.shape
    span = tokens // PARTS
    copies = []
    loads[0].wait()
    for i in range(PARTS):
        here = slice(i * span, (i + 1) * span)
        target = facts_ref[here, 0:1].astype(I32)
        gate, average, inv_std = (facts_ref[here, j : j + 1] for j in (1, 2, 3))
        both = dot(flag(iota((span, back_ref.shape[0]), 1) == target), back_ref[...])
        if i == 0:
            for load in loads[1:]:
                load.wait()
        expert_out, dnormed = both[:, :width], both[:, width:]
        hidden, cot = hidden_ref[here].astype(F32), cot_ref[here].astype(F32)
        block[here] = (hidden + gate * expert_out).astype(BF16)
        dlogit = jnp.sum(cot * expert_out, axis=1, keepdims=True) * gate * (1.0 - gate)
        chosen = flag(iota((span, router_ref.shape[0]), 1) == target // capacity)
        dnormed = dnormed + dlogit * dot(chosen, router_ref[...])
        scaled, xhat = dnormed * gain_ref[...], (hidden - average) * inv_std
        first = jnp.mean(scaled, axis=-1, keepdims=True)
        second = jnp.mean(scaled * xhat, axis=-1, keepdims=True)
        mixer[here] = cot + inv_std * (scaled - first - xhat * second)
        for j, (source, target) in enumerate(((block, block_ref), (mixer, mixer_ref))):
            copies.append(pltpu.make_async_copy(source.at[here], target.at[here], sems.at[i, j]))
            copies[-1].start()
    for copy in copies:
        copy.wait()


def per_device(
    patches,
    patch_mask,
    mask_token,
    w_qkv,
    w_proj,
    logit_scale,
    rel_bias,
    attn_gain,
    moe_gain,
    router,
    expert_ids,
    w_in,
    w_out,
    cotangent,
):
    height, lateral, width = patches.shape
    tokens = height * lateral
    heads = rel_bias.shape[0]
    expert_total = router.shape[1]
    capacity = 2 * tokens // expert_total
    slot_total = expert_total * capacity
    w_in, w_out = w_in[0], w_out[0]
    units = w_in.shape[1]

    dma = pltpu.SemaphoreType.DMA
    cot = cotangent.reshape(tokens, width)
    router_t = router.T
    masked, right, low, corner = call(
        mask_kernel,
        (
            shape((tokens, width), BF16),
            far((height * SHIFT, width), BF16),
            far((SHIFT * lateral, width), BF16),
            far((SHIFT * SHIFT, width), BF16),
        ),
        (FAR, FAR, WHOLE),
        kept_far(patches.reshape(tokens, width)),
        kept_far(patch_mask),
        mask_token,
        scratch=[
            pltpu.VMEM((tokens, width), BF16),
            pltpu.VMEM((height, lateral), I32),
            dma((2,)),
        ],
    )
    right = passed_along(right, "lon", -1)
    low = passed_along(low, "lat", -1)
    corner = passed_diagonally(corner)

    halo_total = (height + lateral + SHIFT) * SHIFT
    target_col, placed, moves, send = call(
        lambda *refs: plan_kernel(expert_total, height, lateral, *refs),
        (
            shape((tokens, 128), I32),
            shape((slot_total, tokens), BF16),
            shape((tokens, tokens + halo_total), BF16),
            far((slot_total, 2 * width), BF16),
        ),
        (FAR, FAR),
        kept_far(expert_ids.reshape(1, tokens)),
        kept_far(cot),
        out_specs=(WHOLE, WHOLE, WHOLE, FAR),
        scratch=[
            pltpu.VMEM((1, tokens), I32),
            pltpu.VMEM((tokens, width), BF16),
            pltpu.VMEM((slot_total, width), BF16),
            dma((2,)),
            dma((PARTS,)),
        ],
        flops=2 * slot_total * tokens * width,
    )
    last = (lax.axis_index("lat") == lax.axis_size("lat") - 1).astype(I32).reshape(1)
    hidden, send = call(
        lambda *refs: attention_kernel(heads, height, lateral, *refs),
        (
            far((tokens, width), BF16),
            far((slot_total, 2 * width), BF16),
        ),
        (SCALAR,) + (WHOLE,) * 6 + (FAR,) * 7,
        last,
        masked,
        right,
        low,
        corner,
        placed,
        moves,
        kept_far(send),
        kept_far(w_qkv),
        kept_far(w_proj),
        kept_far(logit_scale.reshape(1, heads)),
        kept_far(rel_bias),
        kept_far(attn_gain.reshape(1, width)),
        kept_far(moe_gain.reshape(1, width)),
        aliases={7: 1},
        out_specs=(WHOLE, FAR),
        scratch=[
            pltpu.VMEM(w_qkv.shape, BF16),
            pltpu.VMEM(w_proj.shape, BF16),
            pltpu.VMEM((1, heads), F32),
            pltpu.VMEM(rel_bias.shape, F32),
            pltpu.VMEM((1, width), F32),
            pltpu.VMEM((1, width), F32),
            pltpu.VMEM((tokens, width), BF16),
            pltpu.VMEM((slot_total, width), BF16),
            dma((6,)),
            dma((PARTS,)),
        ],
        vmem=32,
        flops=2 * tokens * width * (6 * width + slot_total),
    )
    slots = exchanged(send.reshape(expert_total, capacity, 2 * width)).reshape(
        slot_total, 2 * width
    )
    chunk = units // PARTS
    index = jnp.stack([lax.axis_index("lon"), lax.axis_index("lat")]).astype(I32)
    back, activation, dpre = call(
        expert_kernel,
        (
            far((slot_total, 2 * width), BF16),
            far((slot_total, units), BF16),
            far((slot_total, units), BF16),
        ),
        (SCALAR, WHOLE, WHOLE, FAR, FAR),
        index,
        slots,
        router_t,
        kept_far(w_in),
        kept_far(w_out),
        out_specs=(FAR, FAR, FAR),
        scratch=[
            pltpu.VMEM((width, units), BF16),
            pltpu.VMEM((width, units), BF16),
            pltpu.VMEM((slot_total, units), BF16),
            pltpu.VMEM((slot_total, units), BF16),
            pltpu.VMEM((slot_total, 2 * width), BF16),
            dma((2 * PARTS,)),
            dma((3 * PARTS,)),
        ],
        vmem=40,
        flops=8 * slot_total * width * units,
    )
    back = exchanged(back.reshape(expert_total, capacity, 2 * width)).reshape(
        slot_total, 2 * width
    )

    lat_total = lax.axis_size("lat")
    rows = width // lat_total
    half = width // 2
    keep, give = call(
        lambda *refs: grads_kernel(lat_total, *refs),
        (shape((2, half, units), BF16),) * 2,
        (SCALAR, WHOLE, WHOLE) + (pl.BlockSpec((slot_total, chunk), lambda i: (0, i)),) * 2,
        index,
        slots,
        router_t,
        kept_far(dpre),
        kept_far(activation),
        grid=(PARTS,),
        out_specs=(pl.BlockSpec((2, half, chunk), lambda i: (0, 0, i)),) * 2,
        scratch=[pltpu.VMEM((width, slot_total), BF16)] * 2,
        vmem=28,
        flops=4 * slot_total * width * units,
    )
    given = lax.ppermute(give, "lat", [(i, i ^ 1) for i in range(lat_total)])
    block, part = shape((2, rows, units), BF16), shape((rows, units), BF16)
    own, up, down, up_part, down_part = call(
        pair_kernel, (block, block, block, part, part), (WHOLE,) * 2, keep, given
    )
    up_part = passed_along(up_part, "lat", 2)
    down_part = passed_along(down_part, "lat", -2)
    up, down = call(relay_kernel, (block, block), (WHOLE,) * 4, up, down, up_part, down_part)
    up = passed_along(up, "lat", 2)
    down = passed_along(down, "lat", -2)
    weight_grads = call(
        total_kernel, far((rows, 1, 2 * units), F32), (WHOLE,) * 3, own, up, down
    )
    moe_row = moe_gain.reshape(1, width)
    facts = call(
        lambda *refs: ready_kernel(capacity, *refs),
        far((tokens, 128), F32),
        (WHOLE,) * 4,
        target_col,
        hidden,
        router_t,
        moe_row,
        flops=2 * tokens * slot_total * width,
    )
    block_out, mixer_grad = call(
        lambda *refs: final_kernel(capacity, *refs),
        (far((tokens, width), BF16), far((tokens, width), F32)),
        (UNREAD,) + (FAR,) * 5 + (WHOLE,),
        kept_far(weight_grads),
        kept_far(facts),
        kept_far(hidden),
        kept_far(cot),
        kept_far(router_t),
        kept_far(moe_row),
        back,
        out_specs=(FAR, FAR),
        scratch=[
            pltpu.VMEM((tokens, 128), F32),
            pltpu.VMEM((tokens, width), BF16),
            pltpu.VMEM((tokens, width), BF16),
            pltpu.VMEM((expert_total, width), BF16),
            pltpu.VMEM((1, width), F32),
            pltpu.VMEM((tokens, width), BF16),
            pltpu.VMEM((tokens, width), F32),
            dma((5,)),
            dma((PARTS, 2)),
        ],
        flops=4 * slot_total * tokens * width,
    )
    return (
        block_out.reshape(height, lateral, width),
        mixer_grad.reshape(height, lateral, width),
        weight_grads,
    )


def solution(mesh):
    placed = (
        P("lat", "lon", None),
        P("lat", "lon"),
        P(),
        P(),
        P(),
        P(),
        P(),
        P(),
        P(),
        P(),
        P("lat", "lon", None, None),
        P("lon", None, None),
        P("lon", None, None),
        P("lat", "lon", None),
    )
    return jax.shard_map(
        per_device,
        mesh=mesh,
        in_specs=placed,
        out_specs=(P("lat", "lon", None), P("lat", "lon", None), P("lat", "lon", None)),
        check_vma=False,
    )
```

```python
import math

import jax
import jax.numpy as jnp
from jax import lax
from jax.experimental import pallas as pl
from jax.experimental.pallas import tpu as pltpu
from jax.sharding import PartitionSpec as P

WIN = 8
SHIFT = 4
BF16 = jnp.bfloat16
F32 = jnp.float32
I32 = jnp.int32


MIB = 1024 * 1024
WHOLE = pl.BlockSpec(memory_space=pltpu.VMEM)
SCALAR = pl.BlockSpec(memory_space=pltpu.SMEM)
FAR = pl.BlockSpec(memory_space=pltpu.HBM)
UNREAD = pl.BlockSpec(memory_space=pl.ANY)


def call(
    body, outs, ins, *operands, scratch=(), grid=(), out_specs=None, vmem=16, flops=0, aliases=None
):
    if out_specs is None:
        out_specs = jax.tree.map(lambda _: WHOLE, outs)
    moved = sum(math.prod(x.shape) * x.dtype.itemsize for x in (*operands, *jax.tree.leaves(outs)))
    return pl.pallas_call(
        body,
        grid=grid,
        out_shape=outs,
        in_specs=list(ins),
        out_specs=out_specs,
        scratch_shapes=list(scratch),
        input_output_aliases=aliases or {},
        cost_estimate=pl.CostEstimate(
            flops=int(flops), transcendentals=0, bytes_accessed=int(moved)
        ),
        compiler_params=pltpu.CompilerParams(vmem_limit_bytes=vmem * MIB),
    )(*operands)


def shape(dims, dtype):
    return jax.ShapeDtypeStruct(dims, dtype)


def far(dims, dtype):
    return pltpu.HBM(dims, dtype)


def kept_far(array):
    return pltpu.with_memory_space_constraint(array, pltpu.HBM)


def slot_gates(slots, router_t, index):
    logits = dot_nt(slots, router_t)
    mine = iota(logits.shape, 1) == index
    return jax.nn.sigmoid(jnp.sum(jnp.where(mine, logits, 0.0), axis=1, keepdims=True))


def dot(a, b):
    return jnp.dot(a, b, preferred_element_type=F32)


def dot_nt(a, b):
    return lax.dot_general(a, b, (((1,), (1,)), ((), ())), preferred_element_type=F32)


def dot_tn(a, b):
    return lax.dot_general(a, b, (((0,), (0,)), ((), ())), preferred_element_type=F32)


def halves(values):
    high = values.astype(BF16)
    return high, (values - high.astype(F32)).astype(BF16)


def iota(dims, axis):
    return lax.broadcasted_iota(I32, dims, axis)


def flag(condition):
    return jnp.where(condition, 1.0, 0.0).astype(BF16)


def normal_form(values):
    centred = values - jnp.mean(values, axis=-1, keepdims=True)
    inv_std = lax.rsqrt(jnp.mean(centred * centred, axis=-1, keepdims=True) + 1e-05)
    return centred * inv_std, inv_std


def doubled_gelu_parts(preact):
    scaled = preact * 0.7071067811865476
    doubled_cdf = 1.0 + lax.erf(scaled)
    bell = jnp.exp(-(scaled * scaled))
    return preact * doubled_cdf, doubled_cdf + preact * 0.7978845608028654 * bell


def passed_along(block, axis, distance):
    devices = range(lax.axis_size(axis))
    route = [((i - distance) % len(devices), i) for i in devices]
    return lax.ppermute(block, axis, route)


def passed_diagonally(block):
    rows, columns = lax.axis_size("lat"), lax.axis_size("lon")
    route = [
        ((i + 1) % rows * columns + (j + 1) % columns, i * columns + j)
        for i in range(rows)
        for j in range(columns)
    ]
    return lax.ppermute(block, ("lat", "lon"), route)


def exchanged(slots):
    return lax.all_to_all(slots, "lon", split_axis=0, concat_axis=0, tiled=True)


def send_rows(placed_ref, rows, staged_ref, out_ref, sems):
    copies = []
    step = out_ref.shape[0] // sems.shape[0]
    for i in range(sems.shape[0]):
        part = slice(i * step, (i + 1) * step)
        staged_ref[part] = dot(placed_ref[part], rows).astype(BF16)
        copies.append(pltpu.make_async_copy(staged_ref.at[part], out_ref.at[part], sems.at[i]))
        copies[-1].start()
    return copies


def origins(tokens, height, lateral):
    across = lateral // WIN
    place = iota((tokens, 1), 0)
    which, inside = place // (WIN * WIN), place % (WIN * WIN)
    row = which // across * WIN + inside // WIN + SHIFT
    column = which % across * WIN + inside % WIN + SHIFT
    right_base = tokens
    low_base = right_base + height * SHIFT
    corner_base = low_base + SHIFT * lateral
    local = row * lateral + column
    from_right = right_base + row * SHIFT + column - lateral
    from_low = low_base + (row - height) * lateral + column
    from_corner = corner_base + (row - height) * SHIFT + column - lateral
    return jnp.where(
        row < height,
        jnp.where(column < lateral, local, from_right),
        jnp.where(column < lateral, from_low, from_corner),
    )


def plan_kernel(
    expert_total,
    height,
    lateral,
    ids_far,
    cot_far,
    col_ref,
    placed_ref,
    moves_ref,
    send_ref,
    ids_ref,
    cot_ref,
    staged,
    load_sems,
    sems,
):
    load_ids = pltpu.make_async_copy(ids_far, ids_ref, load_sems.at[0])
    load_cot = pltpu.make_async_copy(cot_far, cot_ref, load_sems.at[1])
    load_ids.start()
    load_cot.start()
    tokens, width = cot_ref.shape
    slot_total = placed_ref.shape[0]
    moves_ref[...] = flag(iota(moves_ref.shape, 1) == origins(tokens, height, lateral))
    before = flag(iota((tokens, tokens), 0) < iota((tokens, tokens), 1))
    load_ids.wait()
    ids = ids_ref[...]
    onehot = iota((expert_total, tokens), 0) == ids
    earlier = dot(flag(onehot), before)
    slot = jnp.sum(jnp.where(onehot, earlier, 0.0), axis=0, keepdims=True).astype(I32)
    target = ids * (slot_total // expert_total) + slot
    placed_ref[...] = flag(iota(placed_ref.shape, 0) == target)
    load_cot.wait()
    copies = send_rows(placed_ref, cot_ref[...], staged, send_ref.at[:, width:], sems)
    diagonal = iota((tokens, tokens), 0) == iota((tokens, tokens), 1)
    column = jnp.sum(jnp.where(diagonal, target, 0).astype(F32), axis=1, keepdims=True)
    col_ref[...] = jnp.broadcast_to(column.astype(I32), col_ref.shape)
    for copy in copies:
        copy.wait()


def mask_kernel(
    patches_ref,
    mask_ref,
    token_ref,
    masked_ref,
    right_ref,
    low_ref,
    corner_ref,
    patches,
    mask,
    token,
    sems,
):
    loads = [
        pltpu.make_async_copy(patches_ref, patches, sems.at[0]),
        pltpu.make_async_copy(mask_ref, mask, sems.at[1]),
        pltpu.make_async_copy(token_ref, token, sems.at[2]),
    ]
    for load in loads:
        load.start()
    for load in loads:
        load.wait()
    tokens = patches_ref.shape[0]
    height, lateral = mask_ref.shape
    in_row = flag(iota((tokens, height), 0) // lateral == iota((tokens, height), 1))
    spread = dot(in_row, mask[...].astype(F32).astype(BF16))
    own = iota((tokens, lateral), 0) % lateral == iota((tokens, lateral), 1)
    hidden_patch = jnp.sum(jnp.where(own, spread, 0.0), axis=1, keepdims=True)
    masked = jnp.where(
        hidden_patch > 0.5, token[...].astype(F32)[None, :], patches[...].astype(F32)
    ).astype(BF16)
    masked_ref[...] = masked
    low_ref[...] = masked[: SHIFT * lateral]
    place = iota((height * SHIFT, tokens), 0)
    picks = flag(place // SHIFT * lateral + place % SHIFT == iota((height * SHIFT, tokens), 1))
    right = dot(picks, masked).astype(BF16)
    right_ref[...] = right
    corner_ref[...] = right[: SHIFT * SHIFT]


def attention_kernel(
    heads,
    height,
    lateral,
    flag_ref,
    masked_ref,
    right_ref,
    low_ref,
    corner_ref,
    placed_ref,
    moves_ref,
    sent_far,
    qkv_far,
    proj_far,
    scale_far,
    bias_far,
    attn_gain_far,
    moe_gain_far,
    hidden_far,
    send_ref,
    hidden_ref,
    qkv_ref,
    proj_ref,
    scale_ref,
    bias_ref,
    attn_gain_ref,
    moe_gain_ref,
    blended_ref,
    staged,
    load_sems,
    sems,
    hidden_sem,
):
    del sent_far
    loads = [
        pltpu.make_async_copy(source, target, load_sems.at[i])
        for i, (source, target) in enumerate(
            (
                (qkv_far, qkv_ref),
                (scale_far, scale_ref),
                (bias_far, bias_ref),
                (proj_far, proj_ref),
                (attn_gain_far, attn_gain_ref),
                (moe_gain_far, moe_gain_ref),
            )
        )
    ]
    for load in loads:
        load.start()
    tokens, width = masked_ref.shape
    features = width // heads
    window = WIN * WIN
    across = lateral // WIN
    group = 128 // features

    source = jnp.concatenate([masked_ref[...], right_ref[...], low_ref[...], corner_ref[...]], axis=0)

    displaced_f = dot(moves_ref[...], source)
    displaced = displaced_f.astype(BF16)

    loads[0].wait()
    projected = dot(displaced, qkv_ref[...]).astype(BF16)
    head_of = flag(iota((width, heads), 0) // features == iota((width, heads), 1))
    of_head = flag(iota((heads, width), 1) // features == iota((heads, width), 0))
    loads[1].wait()
    queries = projected[:, :width].astype(F32)
    keys = projected[:, width : 2 * width].astype(F32)
    query_norm = lax.rsqrt(dot((queries * queries).astype(BF16), head_of) + 1e-06) * scale_ref[...]
    key_norm = lax.rsqrt(dot((keys * keys).astype(BF16), head_of) + 1e-06)
    twice = jnp.concatenate([of_head, of_head], axis=0)
    queries = (queries * dot(jnp.concatenate(halves(query_norm), axis=1), twice)).astype(BF16)
    keys = (keys * dot(jnp.concatenate(halves(key_norm), axis=1), twice)).astype(BF16)

    block = group * window
    loads[2].wait()
    biases = [
        jnp.concatenate([bias_ref[g * group + i] for i in range(group)], axis=1)
        for g in range(width // 128)
    ]
    member = flag(
        iota((block, 128), 0) // window == iota((block, 128), 1) // features
    )
    split = (iota((window, block), 0) >= window // 2) == (
        iota((window, block), 1) % window >= window // 2
    )
    allowed = jnp.where(split, 1.0, jnp.where(flag_ref[0] == 1, 0.0, 1.0))
    groups = width // 128

    def spread(rows, g, start, source):
        part = source[rows, start + g * 128 : start + (g + 1) * 128]
        return jnp.concatenate([part] * group, axis=0) * member

    def score(w):
        rows = slice(w * window, (w + 1) * window)
        return [
            dot_nt(queries[rows, g * 128 : (g + 1) * 128], spread(rows, g, 0, keys)) + biases[g]
            for g in range(groups)
        ]

    def weigh(w, scores):
        weights = [jnp.exp(part) for part in scores]
        if w >= across * (height // WIN - 1):
            weights = [part * allowed for part in weights]
        return [part.astype(BF16) for part in weights]

    def blend(w, weights):
        rows = slice(w * window, (w + 1) * window)
        both = [
            dot(
                weights[g],
                jnp.concatenate([spread(rows, g, 2 * width, projected), member], axis=1),
            )
            for g in range(groups)
        ]
        for g in range(groups):
            part = both[g][:, :128] / both[g][:, 128:]
            blended_ref[rows, g * 128 : (g + 1) * 128] = part.astype(BF16)

    windows = tokens // window
    scores, weights = {}, {}
    for step in range(windows + 2):
        if step < windows:
            scores[step] = score(step)
        if 0 <= step - 1 < windows:
            weights[step - 1] = weigh(step - 1, scores.pop(step - 1))
        if 0 <= step - 2:
            blend(step - 2, weights.pop(step - 2))
    for load in loads[3:]:
        load.wait()
    projection = dot(blended_ref[...], proj_ref[...])
    branch, _ = normal_form(projection)
    hidden = displaced_f + branch * attn_gain_ref[...]
    hidden = hidden.reshape(height // WIN, across, WIN, WIN, width).transpose(0, 2, 1, 3, 4)
    hidden = hidden.reshape(tokens, width).astype(BF16)
    hidden_ref[...] = hidden
    store = pltpu.make_async_copy(hidden_ref, hidden_far, hidden_sem.at[0])
    store.start()
    normed, _ = normal_form(hidden.astype(F32))
    normed = (normed * moe_gain_ref[...]).astype(BF16)
    copies = send_rows(placed_ref, normed, staged, send_ref.at[:, :width], sems)
    for copy in (store, *copies):
        copy.wait()


PARTS = 4
TILES = 4


def expert_kernel(
    index_ref,
    slots_ref,
    router_ref,
    w_in_ref,
    w_out_ref,
    back_ref,
    act_ref,
    dpre_ref,
    w_in,
    w_out,
    act,
    dpre,
    back,
    load_sems,
    store_sems,
):
    rows, width = slots_ref.shape[0], slots_ref.shape[1] // 2
    units = w_in.shape[1]
    tile, chunk, piece = rows // TILES, units // PARTS, width // 2

    def load(source, target, i):
        copy = pltpu.make_async_copy(source, target, load_sems.at[i])
        copy.start()
        return copy

    def tiled(i, step):
        return slice(i * step, (i + 1) * step)

    loads = []
    for i in range(PARTS):
        part = tiled(i, chunk)
        loads.append(load(w_in_ref.at[:, part], w_in.at[:, part], 2 * i))
        loads.append(load(w_out_ref.at[:, part], w_out.at[:, part], 2 * i + 1))
    stores = []

    def store(source, target):
        copy = pltpu.make_async_copy(source, target, store_sems.at[len(stores)])
        copy.start()
        stores.append(copy)

    for r in range(TILES + 1):
        here, last = tiled(r, tile), tiled(r - 1, tile)
        if r == 1:
            half_gate = 0.5 * slot_gates(slots_ref[:, :width], router_ref[...], index_ref[0])
        for c in range(PARTS):
            part = tiled(c, chunk)
            if r < TILES:
                if r == 0:
                    loads[2 * c].wait()
                    loads[2 * c + 1].wait()
                activation, slopes = doubled_gelu_parts(
                    dot(slots_ref[here, :width], w_in[:, part])
                )
                act[here, part] = activation.astype(BF16)
                dact = dot(slots_ref[here, width:], w_out[:, part])
                dpre[here, part] = (dact * slopes).astype(BF16)
            if r > 0:
                half = tiled(c % 2, piece)
                if c < 2:
                    result = 0.5 * dot_nt(act[last], w_out[half])
                else:
                    result = half_gate[last] * dot_nt(dpre[last], w_in[half])
                back[last, tiled(c, piece)] = result.astype(BF16)
        if r < TILES:
            store(act.at[here], act_ref.at[here])
            store(dpre.at[here], dpre_ref.at[here])
        if r > 0:
            store(back.at[last], back_ref.at[last])
    for copy in stores:
        copy.wait()


def grads_kernel(
    lat_total, index_ref, slots_ref, router_ref, dpre_ref, act_ref, keep_ref, give_ref, zt, dt
):
    width = slots_ref.shape[1] // 2
    rows = width // lat_total

    @pl.when(pl.program_id(0) == 0)
    def _():
        place = iota((width, 1), 0)
        half, step, inside = place // (width // 2), place % (width // 2) // rows, place % rows
        column, core = index_ref[1] // 2, index_ref[1] % 2
        block = (step + column) % (lat_total // 2) * 2 + (half + core) % 2
        moves = flag(iota((width, width), 1) == block * rows + inside)
        half_gate = 0.5 * slot_gates(slots_ref[:, :width], router_ref[...], index_ref[0])
        for i, turned in enumerate((zt, dt)):
            part = slots_ref[:, i * width : (i + 1) * width]
            scaled = (part.astype(F32) * half_gate).astype(BF16)
            turned[...] = dot_nt(moves, scaled).astype(BF16)

    for i, (left, right) in enumerate(((zt, dpre_ref), (dt, act_ref))):
        total = dot(left[...], right[...]).astype(BF16)
        keep_ref[i] = total[: width // 2]
        give_ref[i] = total[width // 2 :]


def pair_kernel(keep_ref, given_ref, own_ref, up_ref, down_ref, up_part_ref, down_part_ref):
    rows = own_ref.shape[1]

    def total(i, step):
        part = slice(step * rows, (step + 1) * rows)
        return (keep_ref[i, part].astype(F32) + given_ref[i, part].astype(F32)).astype(BF16)

    for i in range(2):
        own_ref[i] = total(i, 0)
        up_ref[i] = total(i, 1)
        down_ref[i] = total(i, 3)
    up_part_ref[...] = total(0, 2)
    down_part_ref[...] = total(1, 2)


def relay_kernel(up_ref, down_ref, up_part_ref, down_part_ref, up_out_ref, down_out_ref):
    up_out_ref[0] = (up_ref[0].astype(F32) + up_part_ref[...].astype(F32)).astype(BF16)
    up_out_ref[1] = up_ref[1]
    down_out_ref[0] = down_ref[0]
    down_out_ref[1] = (down_ref[1].astype(F32) + down_part_ref[...].astype(F32)).astype(BF16)


def total_kernel(own_ref, up_ref, down_ref, out_ref):
    units = own_ref.shape[2]
    for i in range(2):
        total = own_ref[i].astype(F32) + up_ref[i].astype(F32) + down_ref[i].astype(F32)
        out_ref[:, 0, i * units : (i + 1) * units] = total


def ready_kernel(capacity, col_ref, hidden_ref, router_ref, gain_ref, facts_ref):
    tokens = hidden_ref.shape[0]
    hidden = hidden_ref[...].astype(F32)
    average = jnp.mean(hidden, axis=-1, keepdims=True)
    xhat, inv_std = normal_form(hidden)
    target = col_ref[:, :1]
    chosen = iota((tokens, router_ref.shape[0]), 1) == target // capacity
    logits = dot_nt((xhat * gain_ref[...]).astype(BF16), router_ref[...])
    gate = jax.nn.sigmoid(jnp.sum(jnp.where(chosen, logits, 0.0), axis=1, keepdims=True))
    lane = iota(facts_ref.shape, 1)
    facts_ref[...] = jnp.where(lane == 0, gate, jnp.where(lane == 1, average, inv_std))


def final_kernel(
    capacity,
    grads_ref,
    col_ref,
    facts_far,
    hidden_far,
    cot_far,
    router_far,
    gain_far,
    back_ref,
    block_ref,
    mixer_ref,
    facts_ref,
    hidden_ref,
    cot_ref,
    router_ref,
    gain_ref,
    block,
    mixer,
    load_sems,
    sems,
):
    del grads_ref
    loads = [
        pltpu.make_async_copy(source, target, load_sems.at[i])
        for i, (source, target) in enumerate(
            (
                (facts_far, facts_ref),
                (hidden_far, hidden_ref),
                (cot_far, cot_ref),
                (router_far, router_ref),
                (gain_far, gain_ref),
            )
        )
    ]
    for load in loads:
        load.start()
    tokens, width = hidden_ref.shape
    span = tokens // PARTS
    copies = []
    for i in range(PARTS):
        here = slice(i * span, (i + 1) * span)
        target = col_ref[here, 0:1]
        both = dot(flag(iota((span, back_ref.shape[0]), 1) == target), back_ref[...])
        if i == 0:
            for load in loads:
                load.wait()
        gate, average, inv_std = (facts_ref[here, j : j + 1] for j in range(3))
        expert_out, dnormed = both[:, :width], both[:, width:]
        hidden, cot = hidden_ref[here].astype(F32), cot_ref[here].astype(F32)
        block[here] = (hidden + gate * expert_out).astype(BF16)
        dlogit = jnp.sum(cot * expert_out, axis=1, keepdims=True) * gate * (1.0 - gate)
        chosen = flag(iota((span, router_ref.shape[0]), 1) == target // capacity)
        dnormed = dnormed + dlogit * dot(chosen, router_ref[...])
        scaled, xhat = dnormed * gain_ref[...], (hidden - average) * inv_std
        first = jnp.mean(scaled, axis=-1, keepdims=True)
        second = jnp.mean(scaled * xhat, axis=-1, keepdims=True)
        mixer[here] = cot + inv_std * (scaled - first - xhat * second)
        for j, (source, target) in enumerate(((block, block_ref), (mixer, mixer_ref))):
            copies.append(pltpu.make_async_copy(source.at[here], target.at[here], sems.at[i, j]))
            copies[-1].start()
    for copy in copies:
        copy.wait()


def per_device(
    patches,
    patch_mask,
    mask_token,
    w_qkv,
    w_proj,
    logit_scale,
    rel_bias,
    attn_gain,
    moe_gain,
    router,
    expert_ids,
    w_in,
    w_out,
    cotangent,
):
    height, lateral, width = patches.shape
    tokens = height * lateral
    heads = rel_bias.shape[0]
    expert_total = router.shape[1]
    capacity = 2 * tokens // expert_total
    slot_total = expert_total * capacity
    w_in, w_out = w_in[0], w_out[0]
    units = w_in.shape[1]

    dma = pltpu.SemaphoreType.DMA
    cot = cotangent.reshape(tokens, width)
    router_t = router.T
    masked, right, low, corner = call(
        mask_kernel,
        (
            shape((tokens, width), BF16),
            far((height * SHIFT, width), BF16),
            far((SHIFT * lateral, width), BF16),
            far((SHIFT * SHIFT, width), BF16),
        ),
        (FAR, FAR, FAR),
        kept_far(patches.reshape(tokens, width)),
        kept_far(patch_mask),
        kept_far(mask_token),
        scratch=[
            pltpu.VMEM((tokens, width), BF16),
            pltpu.VMEM((height, lateral), I32),
            pltpu.VMEM((width,), BF16),
            dma((3,)),
        ],
    )
    right = passed_along(right, "lon", -1)
    low = passed_along(low, "lat", -1)
    corner = passed_diagonally(corner)

    halo_total = (height + lateral + SHIFT) * SHIFT
    target_col, placed, moves, send = call(
        lambda *refs: plan_kernel(expert_total, height, lateral, *refs),
        (
            shape((tokens, 128), I32),
            shape((slot_total, tokens), BF16),
            shape((tokens, tokens + halo_total), BF16),
            far((slot_total, 2 * width), BF16),
        ),
        (FAR, FAR),
        kept_far(expert_ids.reshape(1, tokens)),
        kept_far(cot),
        out_specs=(WHOLE, WHOLE, WHOLE, FAR),
        scratch=[
            pltpu.VMEM((1, tokens), I32),
            pltpu.VMEM((tokens, width), BF16),
            pltpu.VMEM((slot_total, width), BF16),
            dma((2,)),
            dma((PARTS,)),
        ],
        flops=2 * slot_total * tokens * width,
    )
    last = (lax.axis_index("lat") == lax.axis_size("lat") - 1).astype(I32).reshape(1)
    hidden, send = call(
        lambda *refs: attention_kernel(heads, height, lateral, *refs),
        (
            far((tokens, width), BF16),
            far((slot_total, 2 * width), BF16),
        ),
        (SCALAR,) + (WHOLE,) * 6 + (FAR,) * 7,
        last,
        masked,
        right,
        low,
        corner,
        placed,
        moves,
        kept_far(send),
        kept_far(w_qkv),
        kept_far(w_proj),
        kept_far(logit_scale.reshape(1, heads)),
        kept_far(rel_bias),
        kept_far(attn_gain.reshape(1, width)),
        kept_far(moe_gain.reshape(1, width)),
        aliases={7: 1},
        out_specs=(FAR, FAR),
        scratch=[
            pltpu.VMEM((tokens, width), BF16),
            pltpu.VMEM(w_qkv.shape, BF16),
            pltpu.VMEM(w_proj.shape, BF16),
            pltpu.VMEM((1, heads), F32),
            pltpu.VMEM(rel_bias.shape, F32),
            pltpu.VMEM((1, width), F32),
            pltpu.VMEM((1, width), F32),
            pltpu.VMEM((tokens, width), BF16),
            pltpu.VMEM((slot_total, width), BF16),
            dma((6,)),
            dma((PARTS,)),
            dma((1,)),
        ],
        vmem=32,
        flops=2 * tokens * width * (6 * width + slot_total),
    )
    slots = exchanged(send.reshape(expert_total, capacity, 2 * width)).reshape(
        slot_total, 2 * width
    )
    chunk = units // PARTS
    index = jnp.stack([lax.axis_index("lon"), lax.axis_index("lat")]).astype(I32)
    back, activation, dpre = call(
        expert_kernel,
        (
            far((slot_total, 2 * width), BF16),
            far((slot_total, units), BF16),
            far((slot_total, units), BF16),
        ),
        (SCALAR, WHOLE, WHOLE, FAR, FAR),
        index,
        slots,
        router_t,
        kept_far(w_in),
        kept_far(w_out),
        out_specs=(FAR, FAR, FAR),
        scratch=[
            pltpu.VMEM((width, units), BF16),
            pltpu.VMEM((width, units), BF16),
            pltpu.VMEM((slot_total, units), BF16),
            pltpu.VMEM((slot_total, units), BF16),
            pltpu.VMEM((slot_total, 2 * width), BF16),
            dma((2 * PARTS,)),
            dma((3 * TILES,)),
        ],
        vmem=40,
        flops=8 * slot_total * width * units,
    )
    back = exchanged(back.reshape(expert_total, capacity, 2 * width)).reshape(
        slot_total, 2 * width
    )

    lat_total = lax.axis_size("lat")
    rows = width // lat_total
    half = width // 2
    keep, give = call(
        lambda *refs: grads_kernel(lat_total, *refs),
        (shape((2, half, units), BF16),) * 2,
        (SCALAR, WHOLE, WHOLE) + (pl.BlockSpec((slot_total, chunk), lambda i: (0, i)),) * 2,
        index,
        slots,
        router_t,
        kept_far(dpre),
        kept_far(activation),
        grid=(PARTS,),
        out_specs=(pl.BlockSpec((2, half, chunk), lambda i: (0, 0, i)),) * 2,
        scratch=[pltpu.VMEM((width, slot_total), BF16)] * 2,
        vmem=28,
        flops=4 * slot_total * width * units,
    )
    given = lax.ppermute(give, "lat", [(i, i ^ 1) for i in range(lat_total)])
    block, part = shape((2, rows, units), BF16), shape((rows, units), BF16)
    own, up, down, up_part, down_part = call(
        pair_kernel, (block, block, block, part, part), (WHOLE,) * 2, keep, given
    )
    up_part = passed_along(up_part, "lat", 2)
    down_part = passed_along(down_part, "lat", -2)
    up, down = call(relay_kernel, (block, block), (WHOLE,) * 4, up, down, up_part, down_part)
    up = passed_along(up, "lat", 2)
    down = passed_along(down, "lat", -2)
    weight_grads = call(
        total_kernel, far((rows, 1, 2 * units), F32), (WHOLE,) * 3, own, up, down
    )
    moe_row = moe_gain.reshape(1, width)
    facts = call(
        lambda *refs: ready_kernel(capacity, *refs),
        far((tokens, 128), F32),
        (WHOLE,) * 4,
        target_col,
        hidden,
        router_t,
        moe_row,
        flops=2 * tokens * slot_total * width,
    )
    block_out, mixer_grad = call(
        lambda *refs: final_kernel(capacity, *refs),
        (far((tokens, width), BF16), far((tokens, width), F32)),
        (UNREAD, WHOLE) + (FAR,) * 5 + (WHOLE,),
        kept_far(weight_grads),
        target_col,
        kept_far(facts),
        kept_far(hidden),
        kept_far(cot),
        kept_far(router_t),
        kept_far(moe_row),
        back,
        out_specs=(FAR, FAR),
        scratch=[
            pltpu.VMEM((tokens, 128), F32),
            pltpu.VMEM((tokens, width), BF16),
            pltpu.VMEM((tokens, width), BF16),
            pltpu.VMEM((expert_total, width), BF16),
            pltpu.VMEM((1, width), F32),
            pltpu.VMEM((tokens, width), BF16),
            pltpu.VMEM((tokens, width), F32),
            dma((5,)),
            dma((PARTS, 2)),
        ],
        flops=4 * slot_total * tokens * width,
    )
    return (
        block_out.reshape(height, lateral, width),
        mixer_grad.reshape(height, lateral, width),
        weight_grads,
    )


def solution(mesh):
    placed = (
        P("lat", "lon", None),
        P("lat", "lon"),
        P(),
        P(),
        P(),
        P(),
        P(),
        P(),
        P(),
        P(),
        P("lat", "lon", None, None),
        P("lon", None, None),
        P("lon", None, None),
        P("lat", "lon", None),
    )
    return jax.shard_map(
        per_device,
        mesh=mesh,
        in_specs=placed,
        out_specs=(P("lat", "lon", None), P("lat", "lon", None), P("lat", "lon", None)),
        check_vma=False,
    )
```

```python
import math

import jax
import jax.numpy as jnp
from jax import lax
from jax.experimental import pallas as pl
from jax.experimental.pallas import tpu as pltpu
from jax.sharding import PartitionSpec as P

WIN = 8
SHIFT = 4
BF16 = jnp.bfloat16
F32 = jnp.float32
I32 = jnp.int32


MIB = 1024 * 1024
WHOLE = pl.BlockSpec(memory_space=pltpu.VMEM)
SCALAR = pl.BlockSpec(memory_space=pltpu.SMEM)
FAR = pl.BlockSpec(memory_space=pltpu.HBM)
UNREAD = pl.BlockSpec(memory_space=pl.ANY)


def call(
    body, outs, ins, *operands, scratch=(), grid=(), out_specs=None, vmem=16, flops=0, aliases=None
):
    if out_specs is None:
        out_specs = jax.tree.map(lambda _: WHOLE, outs)
    moved = sum(math.prod(x.shape) * x.dtype.itemsize for x in (*operands, *jax.tree.leaves(outs)))
    return pl.pallas_call(
        body,
        grid=grid,
        out_shape=outs,
        in_specs=list(ins),
        out_specs=out_specs,
        scratch_shapes=list(scratch),
        input_output_aliases=aliases or {},
        cost_estimate=pl.CostEstimate(
            flops=int(flops), transcendentals=0, bytes_accessed=int(moved)
        ),
        compiler_params=pltpu.CompilerParams(vmem_limit_bytes=vmem * MIB),
    )(*operands)


def shape(dims, dtype):
    return jax.ShapeDtypeStruct(dims, dtype)


def far(dims, dtype):
    return pltpu.HBM(dims, dtype)


def kept_far(array):
    return pltpu.with_memory_space_constraint(array, pltpu.HBM)


def slot_gates(slots, router_t, index):
    logits = dot_nt(slots, router_t)
    mine = iota(logits.shape, 1) == index
    return jax.nn.sigmoid(jnp.sum(jnp.where(mine, logits, 0.0), axis=1, keepdims=True))


def dot(a, b):
    return jnp.dot(a, b, preferred_element_type=F32)


def dot_nt(a, b):
    return lax.dot_general(a, b, (((1,), (1,)), ((), ())), preferred_element_type=F32)


def dot_tn(a, b):
    return lax.dot_general(a, b, (((0,), (0,)), ((), ())), preferred_element_type=F32)


def halves(values):
    high = values.astype(BF16)
    return high, (values - high.astype(F32)).astype(BF16)


def iota(dims, axis):
    return lax.broadcasted_iota(I32, dims, axis)


def flag(condition):
    return jnp.where(condition, 1.0, 0.0).astype(BF16)


def normal_form(values):
    centred = values - jnp.mean(values, axis=-1, keepdims=True)
    inv_std = lax.rsqrt(jnp.mean(centred * centred, axis=-1, keepdims=True) + 1e-05)
    return centred * inv_std, inv_std


def doubled_gelu_parts(preact):
    scaled = preact * 0.7071067811865476
    doubled_cdf = 1.0 + lax.erf(scaled)
    bell = jnp.exp(-(scaled * scaled))
    return preact * doubled_cdf, doubled_cdf + preact * 0.7978845608028654 * bell


def passed_along(block, axis, distance):
    devices = range(lax.axis_size(axis))
    route = [((i - distance) % len(devices), i) for i in devices]
    return lax.ppermute(block, axis, route)


def passed_diagonally(block):
    rows, columns = lax.axis_size("lat"), lax.axis_size("lon")
    route = [
        ((i + 1) % rows * columns + (j + 1) % columns, i * columns + j)
        for i in range(rows)
        for j in range(columns)
    ]
    return lax.ppermute(block, ("lat", "lon"), route)


def exchanged(slots):
    return lax.all_to_all(slots, "lon", split_axis=0, concat_axis=0, tiled=True)


def send_rows(placed_ref, rows, staged_ref, out_ref, sems):
    copies = []
    step = out_ref.shape[0] // sems.shape[0]
    for i in range(sems.shape[0]):
        part = slice(i * step, (i + 1) * step)
        staged_ref[part] = dot(placed_ref[part], rows).astype(BF16)
        copies.append(pltpu.make_async_copy(staged_ref.at[part], out_ref.at[part], sems.at[i]))
        copies[-1].start()
    return copies


def origins(tokens, height, lateral):
    across = lateral // WIN
    place = iota((tokens, 1), 0)
    which, inside = place // (WIN * WIN), place % (WIN * WIN)
    row = which // across * WIN + inside // WIN + SHIFT
    column = which % across * WIN + inside % WIN + SHIFT
    right_base = tokens
    low_base = right_base + height * SHIFT
    corner_base = low_base + SHIFT * lateral
    local = row * lateral + column
    from_right = right_base + row * SHIFT + column - lateral
    from_low = low_base + (row - height) * lateral + column
    from_corner = corner_base + (row - height) * SHIFT + column - lateral
    return jnp.where(
        row < height,
        jnp.where(column < lateral, local, from_right),
        jnp.where(column < lateral, from_low, from_corner),
    )


def plan_kernel(
    expert_total,
    height,
    lateral,
    ids_far,
    cot_far,
    col_ref,
    placed_ref,
    moves_ref,
    send_ref,
    ids_ref,
    cot_ref,
    staged,
    load_sems,
    sems,
):
    load_ids = pltpu.make_async_copy(ids_far, ids_ref, load_sems.at[0])
    load_cot = pltpu.make_async_copy(cot_far, cot_ref, load_sems.at[1])
    load_ids.start()
    load_cot.start()
    tokens, width = cot_ref.shape
    slot_total = placed_ref.shape[0]
    moves_ref[...] = flag(iota(moves_ref.shape, 1) == origins(tokens, height, lateral))
    before = flag(iota((tokens, tokens), 0) < iota((tokens, tokens), 1))
    load_ids.wait()
    ids = ids_ref[...]
    onehot = iota((expert_total, tokens), 0) == ids
    earlier = dot(flag(onehot), before)
    slot = jnp.sum(jnp.where(onehot, earlier, 0.0), axis=0, keepdims=True).astype(I32)
    target = ids * (slot_total // expert_total) + slot
    placed_ref[...] = flag(iota(placed_ref.shape, 0) == target)
    load_cot.wait()
    copies = send_rows(placed_ref, cot_ref[...], staged, send_ref.at[:, width:], sems)
    diagonal = iota((tokens, tokens), 0) == iota((tokens, tokens), 1)
    column = jnp.sum(jnp.where(diagonal, target, 0).astype(F32), axis=1, keepdims=True)
    col_ref[...] = jnp.broadcast_to(column.astype(I32), col_ref.shape)
    for copy in copies:
        copy.wait()


def mask_kernel(
    patches_ref,
    mask_ref,
    token_ref,
    masked_ref,
    right_ref,
    low_ref,
    corner_ref,
    patches,
    mask,
    token,
    sems,
):
    loads = [
        pltpu.make_async_copy(patches_ref, patches, sems.at[0]),
        pltpu.make_async_copy(mask_ref, mask, sems.at[1]),
        pltpu.make_async_copy(token_ref, token, sems.at[2]),
    ]
    for load in loads:
        load.start()
    for load in loads:
        load.wait()
    tokens = patches_ref.shape[0]
    height, lateral = mask_ref.shape
    in_row = flag(iota((tokens, height), 0) // lateral == iota((tokens, height), 1))
    spread = dot(in_row, mask[...].astype(F32).astype(BF16))
    own = iota((tokens, lateral), 0) % lateral == iota((tokens, lateral), 1)
    hidden_patch = jnp.sum(jnp.where(own, spread, 0.0), axis=1, keepdims=True)
    masked = jnp.where(
        hidden_patch > 0.5, token[...].astype(F32)[None, :], patches[...].astype(F32)
    ).astype(BF16)
    masked_ref[...] = masked
    low_ref[...] = masked[: SHIFT * lateral]
    place = iota((height * SHIFT, tokens), 0)
    picks = flag(place // SHIFT * lateral + place % SHIFT == iota((height * SHIFT, tokens), 1))
    right = dot(picks, masked).astype(BF16)
    right_ref[...] = right
    corner_ref[...] = right[: SHIFT * SHIFT]


def attention_kernel(
    heads,
    height,
    lateral,
    flag_ref,
    masked_ref,
    right_ref,
    low_ref,
    corner_ref,
    placed_ref,
    moves_ref,
    sent_far,
    qkv_far,
    proj_far,
    scale_far,
    bias_far,
    attn_gain_far,
    moe_gain_far,
    hidden_far,
    send_ref,
    hidden_ref,
    qkv_ref,
    proj_ref,
    scale_ref,
    bias_ref,
    attn_gain_ref,
    moe_gain_ref,
    blended_ref,
    staged,
    load_sems,
    sems,
    hidden_sem,
):
    del sent_far
    loads = [
        pltpu.make_async_copy(source, target, load_sems.at[i])
        for i, (source, target) in enumerate(
            (
                (qkv_far, qkv_ref),
                (scale_far, scale_ref),
                (bias_far, bias_ref),
                (proj_far, proj_ref),
                (attn_gain_far, attn_gain_ref),
                (moe_gain_far, moe_gain_ref),
            )
        )
    ]
    for load in loads:
        load.start()
    tokens, width = masked_ref.shape
    features = width // heads
    window = WIN * WIN
    across = lateral // WIN
    group = 128 // features

    source = jnp.concatenate([masked_ref[...], right_ref[...], low_ref[...], corner_ref[...]], axis=0)

    displaced_f = dot(moves_ref[...], source)
    displaced = displaced_f.astype(BF16)

    loads[0].wait()
    projected = dot(displaced, qkv_ref[...]).astype(BF16)
    head_of = flag(iota((width, heads), 0) // features == iota((width, heads), 1))
    of_head = flag(iota((heads, width), 1) // features == iota((heads, width), 0))
    loads[1].wait()
    queries = projected[:, :width].astype(F32)
    keys = projected[:, width : 2 * width].astype(F32)
    query_norm = lax.rsqrt(dot((queries * queries).astype(BF16), head_of) + 1e-06) * scale_ref[...]
    key_norm = lax.rsqrt(dot((keys * keys).astype(BF16), head_of) + 1e-06)
    twice = jnp.concatenate([of_head, of_head], axis=0)
    queries = (queries * dot(jnp.concatenate(halves(query_norm), axis=1), twice)).astype(BF16)
    keys = (keys * dot(jnp.concatenate(halves(key_norm), axis=1), twice)).astype(BF16)

    block = group * window
    loads[2].wait()
    biases = [
        jnp.concatenate([bias_ref[g * group + i] for i in range(group)], axis=1)
        for g in range(width // 128)
    ]
    member = flag(
        iota((block, 128), 0) // window == iota((block, 128), 1) // features
    )
    split = (iota((window, block), 0) >= window // 2) == (
        iota((window, block), 1) % window >= window // 2
    )
    allowed = jnp.where(split, 1.0, jnp.where(flag_ref[0] == 1, 0.0, 1.0))
    groups = width // 128

    def spread(rows, g, start, source):
        part = source[rows, start + g * 128 : start + (g + 1) * 128]
        return jnp.concatenate([part] * group, axis=0) * member

    def score(w):
        rows = slice(w * window, (w + 1) * window)
        return [
            dot_nt(queries[rows, g * 128 : (g + 1) * 128], spread(rows, g, 0, keys)) + biases[g]
            for g in range(groups)
        ]

    def weigh(w, scores):
        weights = [jnp.exp(part) for part in scores]
        if w >= across * (height // WIN - 1):
            weights = [part * allowed for part in weights]
        return [part.astype(BF16) for part in weights]

    def blend(w, weights):
        rows = slice(w * window, (w + 1) * window)
        both = [
            dot(
                weights[g],
                jnp.concatenate([spread(rows, g, 2 * width, projected), member], axis=1),
            )
            for g in range(groups)
        ]
        for g in range(groups):
            part = both[g][:, :128] / both[g][:, 128:]
            blended_ref[rows, g * 128 : (g + 1) * 128] = part.astype(BF16)

    windows = tokens // window
    scores, weights = {}, {}
    for step in range(windows + 2):
        if step < windows:
            scores[step] = score(step)
        if 0 <= step - 1 < windows:
            weights[step - 1] = weigh(step - 1, scores.pop(step - 1))
        if 0 <= step - 2:
            blend(step - 2, weights.pop(step - 2))
    for load in loads[3:]:
        load.wait()
    projection = dot(blended_ref[...], proj_ref[...])
    branch, _ = normal_form(projection)
    hidden = displaced_f + branch * attn_gain_ref[...]
    hidden = hidden.reshape(height // WIN, across, WIN, WIN, width).transpose(0, 2, 1, 3, 4)
    hidden = hidden.reshape(tokens, width).astype(BF16)
    hidden_ref[...] = hidden
    store = pltpu.make_async_copy(hidden_ref, hidden_far, hidden_sem.at[0])
    store.start()
    normed, _ = normal_form(hidden.astype(F32))
    normed = (normed * moe_gain_ref[...]).astype(BF16)
    copies = send_rows(placed_ref, normed, staged, send_ref.at[:, :width], sems)
    for copy in (store, *copies):
        copy.wait()


PARTS = 4
TILES = 4


def expert_kernel(
    index_ref,
    slots_ref,
    router_ref,
    w_in,
    w_out,
    back_ref,
    act_ref,
    dpre_ref,
    act,
    dpre,
    back,
    store_sems,
):
    rows, width = slots_ref.shape[0], slots_ref.shape[1] // 2
    units = w_in.shape[1]
    tile, chunk, piece = rows // TILES, units // PARTS, width // 2

    def tiled(i, step):
        return slice(i * step, (i + 1) * step)

    stores = []

    def store(source, target):
        copy = pltpu.make_async_copy(source, target, store_sems.at[len(stores)])
        copy.start()
        stores.append(copy)

    for r in range(TILES + 1):
        here, last = tiled(r, tile), tiled(r - 1, tile)
        if r == 1:
            half_gate = 0.5 * slot_gates(slots_ref[:, :width], router_ref[...], index_ref[0])
        for c in range(PARTS):
            part = tiled(c, chunk)
            if r < TILES:
                activation, slopes = doubled_gelu_parts(
                    dot(slots_ref[here, :width], w_in[:, part])
                )
                act[here, part] = activation.astype(BF16)
                dact = dot(slots_ref[here, width:], w_out[:, part])
                dpre[here, part] = (dact * slopes).astype(BF16)
            if r > 0:
                half = tiled(c % 2, piece)
                if c < 2:
                    result = 0.5 * dot_nt(act[last], w_out[half])
                else:
                    result = half_gate[last] * dot_nt(dpre[last], w_in[half])
                back[last, tiled(c, piece)] = result.astype(BF16)
        if r < TILES:
            store(act.at[here], act_ref.at[here])
            store(dpre.at[here], dpre_ref.at[here])
        if r > 0:
            store(back.at[last], back_ref.at[last])
    for copy in stores:
        copy.wait()


def grads_kernel(
    lat_total, index_ref, slots_ref, router_ref, dpre_ref, act_ref, keep_ref, give_ref, zt, dt
):
    width = slots_ref.shape[1] // 2
    rows = width // lat_total

    @pl.when(pl.program_id(0) == 0)
    def _():
        place = iota((width, 1), 0)
        half, step, inside = place // (width // 2), place % (width // 2) // rows, place % rows
        column, core = index_ref[1] // 2, index_ref[1] % 2
        block = (step + column) % (lat_total // 2) * 2 + (half + core) % 2
        moves = flag(iota((width, width), 1) == block * rows + inside)
        half_gate = 0.5 * slot_gates(slots_ref[:, :width], router_ref[...], index_ref[0])
        for i, turned in enumerate((zt, dt)):
            part = slots_ref[:, i * width : (i + 1) * width]
            scaled = (part.astype(F32) * half_gate).astype(BF16)
            turned[...] = dot_nt(moves, scaled).astype(BF16)

    for i, (left, right) in enumerate(((zt, dpre_ref), (dt, act_ref))):
        total = dot(left[...], right[...]).astype(BF16)
        keep_ref[i] = total[: width // 2]
        give_ref[i] = total[width // 2 :]


def pair_kernel(keep_ref, given_ref, own_ref, up_ref, down_ref, up_part_ref, down_part_ref):
    rows = own_ref.shape[1]

    def total(i, step):
        part = slice(step * rows, (step + 1) * rows)
        return (keep_ref[i, part].astype(F32) + given_ref[i, part].astype(F32)).astype(BF16)

    for i in range(2):
        own_ref[i] = total(i, 0)
        up_ref[i] = total(i, 1)
        down_ref[i] = total(i, 3)
    up_part_ref[...] = total(0, 2)
    down_part_ref[...] = total(1, 2)


def relay_kernel(up_ref, down_ref, up_part_ref, down_part_ref, up_out_ref, down_out_ref):
    up_out_ref[0] = (up_ref[0].astype(F32) + up_part_ref[...].astype(F32)).astype(BF16)
    up_out_ref[1] = up_ref[1]
    down_out_ref[0] = down_ref[0]
    down_out_ref[1] = (down_ref[1].astype(F32) + down_part_ref[...].astype(F32)).astype(BF16)


def total_kernel(own_ref, up_ref, down_ref, out_ref):
    units = own_ref.shape[2]
    for i in range(2):
        total = own_ref[i].astype(F32) + up_ref[i].astype(F32) + down_ref[i].astype(F32)
        out_ref[:, 0, i * units : (i + 1) * units] = total


def ready_kernel(capacity, col_ref, hidden_ref, router_ref, gain_ref, facts_ref):
    tokens = hidden_ref.shape[0]
    hidden = hidden_ref[...].astype(F32)
    average = jnp.mean(hidden, axis=-1, keepdims=True)
    xhat, inv_std = normal_form(hidden)
    target = col_ref[:, :1]
    chosen = iota((tokens, router_ref.shape[0]), 1) == target // capacity
    logits = dot_nt((xhat * gain_ref[...]).astype(BF16), router_ref[...])
    gate = jax.nn.sigmoid(jnp.sum(jnp.where(chosen, logits, 0.0), axis=1, keepdims=True))
    lane = iota(facts_ref.shape, 1)
    facts_ref[...] = jnp.where(lane == 0, gate, jnp.where(lane == 1, average, inv_std))


def final_kernel(
    capacity,
    grads_ref,
    col_ref,
    facts_far,
    hidden_far,
    cot_far,
    router_far,
    gain_far,
    back_ref,
    block_ref,
    mixer_ref,
    facts_ref,
    hidden_ref,
    cot_ref,
    router_ref,
    gain_ref,
    block,
    mixer,
    load_sems,
    sems,
):
    del grads_ref
    loads = [
        pltpu.make_async_copy(source, target, load_sems.at[i])
        for i, (source, target) in enumerate(
            (
                (facts_far, facts_ref),
                (hidden_far, hidden_ref),
                (cot_far, cot_ref),
                (router_far, router_ref),
                (gain_far, gain_ref),
            )
        )
    ]
    for load in loads:
        load.start()
    tokens, width = hidden_ref.shape
    span = tokens // PARTS
    copies = []
    for i in range(PARTS):
        here = slice(i * span, (i + 1) * span)
        target = col_ref[here, 0:1]
        both = dot(flag(iota((span, back_ref.shape[0]), 1) == target), back_ref[...])
        if i == 0:
            for load in loads:
                load.wait()
        gate, average, inv_std = (facts_ref[here, j : j + 1] for j in range(3))
        expert_out, dnormed = both[:, :width], both[:, width:]
        hidden, cot = hidden_ref[here].astype(F32), cot_ref[here].astype(F32)
        block[here] = (hidden + gate * expert_out).astype(BF16)
        dlogit = jnp.sum(cot * expert_out, axis=1, keepdims=True) * gate * (1.0 - gate)
        chosen = flag(iota((span, router_ref.shape[0]), 1) == target // capacity)
        dnormed = dnormed + dlogit * dot(chosen, router_ref[...])
        scaled, xhat = dnormed * gain_ref[...], (hidden - average) * inv_std
        first = jnp.mean(scaled, axis=-1, keepdims=True)
        second = jnp.mean(scaled * xhat, axis=-1, keepdims=True)
        mixer[here] = cot + inv_std * (scaled - first - xhat * second)
        for j, (source, target) in enumerate(((block, block_ref), (mixer, mixer_ref))):
            copies.append(pltpu.make_async_copy(source.at[here], target.at[here], sems.at[i, j]))
            copies[-1].start()
    for copy in copies:
        copy.wait()


def per_device(
    patches,
    patch_mask,
    mask_token,
    w_qkv,
    w_proj,
    logit_scale,
    rel_bias,
    attn_gain,
    moe_gain,
    router,
    expert_ids,
    w_in,
    w_out,
    cotangent,
):
    height, lateral, width = patches.shape
    tokens = height * lateral
    heads = rel_bias.shape[0]
    expert_total = router.shape[1]
    capacity = 2 * tokens // expert_total
    slot_total = expert_total * capacity
    w_in, w_out = w_in[0], w_out[0]
    units = w_in.shape[1]

    dma = pltpu.SemaphoreType.DMA
    cot = cotangent.reshape(tokens, width)
    router_t = router.T
    masked, right, low, corner = call(
        mask_kernel,
        (
            shape((tokens, width), BF16),
            far((height * SHIFT, width), BF16),
            far((SHIFT * lateral, width), BF16),
            far((SHIFT * SHIFT, width), BF16),
        ),
        (FAR, FAR, FAR),
        kept_far(patches.reshape(tokens, width)),
        kept_far(patch_mask),
        kept_far(mask_token),
        scratch=[
            pltpu.VMEM((tokens, width), BF16),
            pltpu.VMEM((height, lateral), I32),
            pltpu.VMEM((width,), BF16),
            dma((3,)),
        ],
    )
    right = passed_along(right, "lon", -1)
    low = passed_along(low, "lat", -1)
    corner = passed_diagonally(corner)

    halo_total = (height + lateral + SHIFT) * SHIFT
    target_col, placed, moves, send = call(
        lambda *refs: plan_kernel(expert_total, height, lateral, *refs),
        (
            shape((tokens, 128), I32),
            shape((slot_total, tokens), BF16),
            shape((tokens, tokens + halo_total), BF16),
            far((slot_total, 2 * width), BF16),
        ),
        (FAR, FAR),
        kept_far(expert_ids.reshape(1, tokens)),
        kept_far(cot),
        out_specs=(WHOLE, WHOLE, WHOLE, FAR),
        scratch=[
            pltpu.VMEM((1, tokens), I32),
            pltpu.VMEM((tokens, width), BF16),
            pltpu.VMEM((slot_total, width), BF16),
            dma((2,)),
            dma((PARTS,)),
        ],
        flops=2 * slot_total * tokens * width,
    )
    last = (lax.axis_index("lat") == lax.axis_size("lat") - 1).astype(I32).reshape(1)
    hidden, send = call(
        lambda *refs: attention_kernel(heads, height, lateral, *refs),
        (
            far((tokens, width), BF16),
            far((slot_total, 2 * width), BF16),
        ),
        (SCALAR,) + (WHOLE,) * 6 + (FAR,) * 7,
        last,
        masked,
        right,
        low,
        corner,
        placed,
        moves,
        kept_far(send),
        kept_far(w_qkv),
        kept_far(w_proj),
        kept_far(logit_scale.reshape(1, heads)),
        kept_far(rel_bias),
        kept_far(attn_gain.reshape(1, width)),
        kept_far(moe_gain.reshape(1, width)),
        aliases={7: 1},
        out_specs=(FAR, FAR),
        scratch=[
            pltpu.VMEM((tokens, width), BF16),
            pltpu.VMEM(w_qkv.shape, BF16),
            pltpu.VMEM(w_proj.shape, BF16),
            pltpu.VMEM((1, heads), F32),
            pltpu.VMEM(rel_bias.shape, F32),
            pltpu.VMEM((1, width), F32),
            pltpu.VMEM((1, width), F32),
            pltpu.VMEM((tokens, width), BF16),
            pltpu.VMEM((slot_total, width), BF16),
            dma((6,)),
            dma((PARTS,)),
            dma((1,)),
        ],
        vmem=32,
        flops=2 * tokens * width * (6 * width + slot_total),
    )
    slots = exchanged(send.reshape(expert_total, capacity, 2 * width)).reshape(
        slot_total, 2 * width
    )
    chunk = units // PARTS
    index = jnp.stack([lax.axis_index("lon"), lax.axis_index("lat")]).astype(I32)
    back, activation, dpre = call(
        expert_kernel,
        (
            far((slot_total, 2 * width), BF16),
            far((slot_total, units), BF16),
            far((slot_total, units), BF16),
        ),
        (SCALAR,) + (WHOLE,) * 4,
        index,
        slots,
        router_t,
        w_in,
        w_out,
        out_specs=(FAR, FAR, FAR),
        scratch=[
            pltpu.VMEM((slot_total, units), BF16),
            pltpu.VMEM((slot_total, units), BF16),
            pltpu.VMEM((slot_total, 2 * width), BF16),
            dma((3 * TILES,)),
        ],
        vmem=32,
        flops=8 * slot_total * width * units,
    )
    back = exchanged(back.reshape(expert_total, capacity, 2 * width)).reshape(
        slot_total, 2 * width
    )

    lat_total = lax.axis_size("lat")
    rows = width // lat_total
    half = width // 2
    keep, give = call(
        lambda *refs: grads_kernel(lat_total, *refs),
        (shape((2, half, units), BF16),) * 2,
        (SCALAR, WHOLE, WHOLE) + (pl.BlockSpec((slot_total, chunk), lambda i: (0, i)),) * 2,
        index,
        slots,
        router_t,
        kept_far(dpre),
        kept_far(activation),
        grid=(PARTS,),
        out_specs=(pl.BlockSpec((2, half, chunk), lambda i: (0, 0, i)),) * 2,
        scratch=[pltpu.VMEM((width, slot_total), BF16)] * 2,
        vmem=28,
        flops=4 * slot_total * width * units,
    )
    given = lax.ppermute(give, "lat", [(i, i ^ 1) for i in range(lat_total)])
    block, part = shape((2, rows, units), BF16), shape((rows, units), BF16)
    own, up, down, up_part, down_part = call(
        pair_kernel, (block, block, block, part, part), (WHOLE,) * 2, keep, given
    )
    up_part = passed_along(up_part, "lat", 2)
    down_part = passed_along(down_part, "lat", -2)
    up, down = call(relay_kernel, (block, block), (WHOLE,) * 4, up, down, up_part, down_part)
    up = passed_along(up, "lat", 2)
    down = passed_along(down, "lat", -2)
    weight_grads = call(
        total_kernel, far((rows, 1, 2 * units), F32), (WHOLE,) * 3, own, up, down
    )
    moe_row = moe_gain.reshape(1, width)
    facts = call(
        lambda *refs: ready_kernel(capacity, *refs),
        far((tokens, 128), F32),
        (WHOLE,) * 4,
        target_col,
        hidden,
        router_t,
        moe_row,
        flops=2 * tokens * slot_total * width,
    )
    block_out, mixer_grad = call(
        lambda *refs: final_kernel(capacity, *refs),
        (far((tokens, width), BF16), far((tokens, width), F32)),
        (UNREAD, WHOLE) + (FAR,) * 5 + (WHOLE,),
        kept_far(weight_grads),
        target_col,
        kept_far(facts),
        kept_far(hidden),
        kept_far(cot),
        kept_far(router_t),
        kept_far(moe_row),
        back,
        out_specs=(FAR, FAR),
        scratch=[
            pltpu.VMEM((tokens, 128), F32),
            pltpu.VMEM((tokens, width), BF16),
            pltpu.VMEM((tokens, width), BF16),
            pltpu.VMEM((expert_total, width), BF16),
            pltpu.VMEM((1, width), F32),
            pltpu.VMEM((tokens, width), BF16),
            pltpu.VMEM((tokens, width), F32),
            dma((5,)),
            dma((PARTS, 2)),
        ],
        flops=4 * slot_total * tokens * width,
    )
    return (
        block_out.reshape(height, lateral, width),
        mixer_grad.reshape(height, lateral, width),
        weight_grads,
    )


def solution(mesh):
    placed = (
        P("lat", "lon", None),
        P("lat", "lon"),
        P(),
        P(),
        P(),
        P(),
        P(),
        P(),
        P(),
        P(),
        P("lat", "lon", None, None),
        P("lon", None, None),
        P("lon", None, None),
        P("lat", "lon", None),
    )
    return jax.shard_map(
        per_device,
        mesh=mesh,
        in_specs=placed,
        out_specs=(P("lat", "lon", None), P("lat", "lon", None), P("lat", "lon", None)),
        check_vma=False,
    )
```
